256 devices in a mesh: replica: 8 (over x, core), fsdp: 32 (over y, z).
Axes of the slice: x: 4, y: 4, z: 8, core: 2. Of those that a mesh axis runs over, the one named last changes fastest.
Arguments:
- delta: bfloat16 [8, 2, 1536, 5120], P('replica', None, 'fsdp'), may hold values from -6 to 6
- error: bfloat16 [8, 2, 1536, 5120], P('replica', None, None, 'fsdp'), may hold values from -6 to 6
- theta: float32 [2, 1536, 5120], P(None, 'fsdp'), may hold values from -6 to 6
- momentum: float32 [2, 1536, 5120], P(None, 'fsdp'), may hold values from -4 to 4
- block_index: int32 [8, 480, 16], P('replica', 'fsdp'), may hold values from 0 to 255, as said below
- block_count: int32 [8, 480], P('replica', 'fsdp'), may hold values from 1 to 16
Outputs:
- theta_new: float32 [2, 1536, 5120], P(None, 'fsdp')
- momentum_new: float32 [2, 1536, 5120], P(None, 'fsdp')
- error_new: bfloat16 [8, 2, 1536, 5120], P('replica', None, None, 'fsdp')
The draws below stay inside these ranges and needn't reach their ends.
Inputs may be any that keep to these rules, and one draw needn't show every extreme that they name: The first block_count[r, g] entries of each list block_index[r, g, :] are distinct; the remaining entries are padding.
All inputs are finite; a program needn't handle non-finite values.
Results may differ from the reference program's by a relative error of at most 0.0033.
Values may be sent and summed in bfloat16 or wider, within the bound.
A program may use at most 64 MiB of HBM per device.

```python
import jax
import jax.numpy as jnp
from jax import lax

D = 5120
FF = 1536
EXPERTS = 2
SPAN = 256
GROUP = 128
CAP = 16
REPLICAS = 8
COLS = 160
GROUPS = 480
GROUPS_DEV = 15
N_FSDP = 32


def draw_block_index(key, part):
    key = jax.random.fold_in(key, 11)
    scores = jax.random.randint(key, (REPLICAS, GROUPS, SPAN), 0, 2 ** 20) * SPAN + jnp.arange(SPAN, dtype=jnp.int32)
    ranking = jnp.argsort(scores, axis=-1, stable=True)
    return ranking[:, :, :CAP].astype(jnp.int32)


def draw_block_count(key, part):
    key = jax.random.fold_in(key, 23)
    level_key, short_key, full_key = jax.random.split(key, 3)
    column_ranges = GROUPS // GROUPS_DEV
    level_draw = jax.random.randint(level_key, (REPLICAS, column_ranges, 1), 1, 5)
    shortfall = jax.random.randint(short_key, (REPLICAS, column_ranges, GROUPS_DEV), 0, max(CAP // 4, 1))
    counts = jnp.maximum(level_draw * (CAP // 4) - shortfall, 1)
    full_slot = jax.random.randint(full_key, (REPLICAS, column_ranges, 1), 0, GROUPS_DEV)
    positions = jnp.arange(GROUPS_DEV, dtype=jnp.int32)[None, None, :]
    counts = jnp.where(positions == full_slot, CAP, counts)
    return counts.reshape(REPLICAS, GROUPS).astype(jnp.int32)


def block_levels(key, extent, cuts, smallest, largest):
    def one(position, parts):
        draws = jax.random.uniform(jax.random.fold_in(jax.random.fold_in(key, 6), position), (parts,), jnp.float32, smallest / len(cuts), largest / len(cuts))
        return jnp.repeat(jnp.exp(draws), extent[position] // parts).reshape((-1,) + (1,) * (len(extent) - position - 1))

    factor_of = one(*cuts[0])
    for cut in cuts[1:]:
        factor_of = factor_of * one(*cut)
    return factor_of


def normal_values(key, shape, spread, bound, pieces=(), kind=jnp.bfloat16):
    result = spread * jax.random.normal(key, shape, jnp.float32)
    if pieces:
        result = result * block_levels(key, shape, pieces, -0.22, 0.18)
    return jnp.clip(result, -bound, bound).astype(kind)


def setup_inputs(seed: int = 0) -> dict:
    seeds = jax.random.split(jax.random.key(seed), 7)
    return {
        "delta": normal_values(seeds[0], (REPLICAS, EXPERTS, FF, D), 1.0, 6.0, ((0, 8), (2, 32))),
        "error": normal_values(seeds[1], (REPLICAS, EXPERTS, FF, D), 1.0, 6.0, ((0, 8), (3, 32))),
        "theta": normal_values(seeds[2], (EXPERTS, FF, D), 1.0, 6.0, ((1, 32),), jnp.float32),
        "momentum": normal_values(seeds[3], (EXPERTS, FF, D), 0.3, 4.0, ((1, 32),), jnp.float32),
        "block_index": draw_block_index(jax.random.fold_in(seeds[6], 71), 0),
        "block_count": draw_block_count(jax.random.fold_in(seeds[6], 71), 0),
    }


error_decay = 0.95
outer_momentum = 0.9
outer_rate = 0.7

def make_cosines(length):
    freqs = jnp.arange(length, dtype=jnp.float32)[:, None]
    places = jnp.arange(length, dtype=jnp.float32)[None, :]
    angles = jnp.cos(jnp.pi * (2.0 * places + 1.0) * freqs / (2.0 * length))
    scaling = jnp.where(freqs == 0, jnp.sqrt(1.0 / length), jnp.sqrt(2.0 / length))
    return angles * scaling

def to_blocks(field):
    shaped = field.reshape(EXPERTS, FF // SPAN, SPAN, N_FSDP, COLS)
    shaped = jnp.transpose(shaped, (2, 3, 0, 1, 4))
    return shaped.reshape(SPAN, GROUPS, GROUP)

def from_blocks(blocks):
    shaped = blocks.reshape(SPAN, N_FSDP, EXPERTS, FF // SPAN, COLS)
    shaped = jnp.transpose(shaped, (2, 3, 0, 1, 4))
    return shaped.reshape(EXPERTS, FF, D)

def reference(delta, error, theta, momentum, block_index, block_count):
    cosines = make_cosines(SPAN)
    highest = lax.Precision.HIGHEST

    def one_replica(summed, inputs):
        delta_one, error_one, index_one, count_one = inputs
        carried = error_decay * error_one.astype(jnp.float32) + delta_one.astype(jnp.float32)
        spectrum = jnp.einsum('kt,tgn->kgn', cosines, to_blocks(carried), precision=highest)
        live_slots = jnp.arange(CAP, dtype=jnp.int32)[None, :] < count_one[:, None]
        matches = (index_one[:, :, None] == jnp.arange(SPAN, dtype=jnp.int32)[None, None, :]) & live_slots[:, :, None]
        chosen = jnp.transpose(jnp.any(matches, axis=1).astype(jnp.float32))[:, :, None]
        kept_half = lax.optimization_barrier((spectrum * chosen).astype(jnp.bfloat16))
        kept = kept_half.astype(jnp.float32)
        restored = from_blocks(jnp.einsum('kt,kgn->tgn', cosines, kept, precision=highest))
        error_out = (carried - restored).astype(jnp.bfloat16)
        return (summed + kept, error_out)
    start_sum = jnp.zeros((SPAN, GROUPS, GROUP), jnp.float32)
    summed, error_new = lax.scan(one_replica, start_sum, (delta, error, block_index, block_count))
    averaged = summed / REPLICAS
    update = from_blocks(jnp.einsum('kt,kgn->tgn', cosines, averaged, precision=highest))
    momentum_new = outer_momentum * momentum + update
    theta_new = theta - outer_rate * (update + outer_momentum * momentum_new)
    return (theta_new, momentum_new, error_new)
```

```python
import jax
import jax.numpy as jnp
import numpy as np
from jax import lax
from jax.experimental import pallas as pl
from jax.experimental.pallas import tpu as pltpu
from jax.sharding import PartitionSpec as P

SPAN = 256
N = 32
R = 8
ROWS = 48
MESH = pl.DeviceIdType.MESH
F32 = jnp.float32
BF16 = jnp.bfloat16
I32 = jnp.int32


def cosine_parts():
    k = np.arange(SPAN, dtype=np.float64)[:, None]
    t = np.arange(SPAN, dtype=np.float64)[None, :]
    m = np.cos(np.pi * (2.0 * t + 1.0) * k / (2.0 * SPAN))
    m = m * np.where(k == 0, np.sqrt(1.0 / SPAN), np.sqrt(2.0 / SPAN))
    hi = m.astype(jnp.bfloat16)
    lo = (m - hi.astype(np.float64)).astype(jnp.bfloat16)
    return np.stack([hi, lo, hi.T, lo.T])


def div(a, b):
    return lax.div(a, jnp.int32(b))


def rem(a, b):
    return lax.rem(a, jnp.int32(b))


def owner_of(f):
    y, z = div(f, 8), rem(f, 8)
    return 2 * rem(y + z, 4) + div(z, 4)


def dot_nt(a, b):
    return lax.dot_general(a, b, (((1,), (1,)), ((), ())), preferred_element_type=F32)


def dot_tn(a, b):
    return lax.dot_general(a, b, (((0,), (0,)), ((), ())), preferred_element_type=F32)


def dot(a, b):
    return jnp.dot(a, b, preferred_element_type=F32)


def lanes(shape):
    return lax.broadcasted_iota(I32, shape, len(shape) - 1)


def exchange_kernel(
    delta, err, cos, own_idx, flat_idx,
    upd, upd_tail, err_out,
    d_v, e_v, cos_v, send, send_t, recv, recv_t, x_t, low, basis,
    idx_all, kept, kept_all, u_out, u_tail, u_msg, u_recv,
    load_sem, a2a_s, a2a_r, idx_s, idx_r, kept_s, kept_r, upd_s, upd_r, fwd_s, fwd_r,
):
    r = lax.axis_index("replica")
    f = lax.axis_index("fsdp")
    y, z = div(f, 8), rem(f, 8)
    fm = rem(f, 4)
    own = owner_of(f)
    is_owner = r == own

    loads = [
        pltpu.make_async_copy(delta.at[0], d_v.at[0], load_sem.at[0]),
        pltpu.make_async_copy(delta.at[1], d_v.at[1], load_sem.at[1]),
        pltpu.make_async_copy(cos, cos_v, load_sem.at[2]),
        pltpu.make_async_copy(err, e_v, load_sem.at[3]),
    ]
    for c in loads:
        c.start()

    bar = pltpu.get_barrier_semaphore()

    def greet_row(o, _):
        pl.semaphore_signal(bar, inc=1, device_id=(r, rem(f + o, N)), device_id_type=MESH)
        return 0

    def greet_col(o, _):
        pl.semaphore_signal(bar, inc=1, device_id=(rem(r + o, R), f), device_id_type=MESH)
        return 0

    lax.fori_loop(1, N, greet_row, 0)
    lax.fori_loop(1, R, greet_col, 0)

    lane16 = lanes((16, 128))

    def pack_main(e):
        def body(q, _):
            for i in range(3):
                rows = pl.ds(16 * i, 16)
                t = [
                    d_v[e, rows, pl.ds(pl.multiple_of(640 * q + 128 * k, 128), 128)]
                    for k in range(5)
                ]
                send[e, 4 * q, rows] = t[0]
                send[e, 4 * q + 1, rows] = jnp.where(lane16 >= 32, t[1], t[2])
                send[e, 4 * q + 2, rows] = jnp.where(lane16 >= 64, t[2], t[3])
                send[e, 4 * q + 3, rows] = jnp.where(lane16 >= 96, t[3], t[4])
            return 0

        lax.fori_loop(0, 8, body, 0)

    def pack_tail():
        def body(q, _):
            zs = []
            for g in range(6):
                e, i = g // 3, g % 3
                t = [
                    d_v[e, 16 * i:16 * i + 16, pl.ds(pl.multiple_of(640 * q + 128 * k, 128), 128)]
                    for k in range(1, 5)
                ]
                v = jnp.where(
                    lane16 < 32, t[0], jnp.where(lane16 < 64, t[1], jnp.where(lane16 < 96, t[2], t[3]))
                )
                zs.append(v.astype(F32))
            for m in range(4):
                w = [None, None]
                for g in range(6):
                    k = g % 4
                    s = (32 * (k - m)) % 128
                    v = pltpu.roll(zs[g], s, 1) if s else zs[g]
                    p = w[g // 4]
                    w[g // 4] = v if p is None else jnp.where(lane16 < 32 * k, p, v)
                send_t[4 * q + m, 0:16] = w[0].astype(BF16)
                send_t[4 * q + m, 16:32] = w[1].astype(BF16)
            return 0

        lax.fori_loop(0, 8, body, 0)

    def send_main(e):
        def body(o, _):
            d = rem(f + o, N)
            pltpu.make_async_remote_copy(
                src_ref=send.at[e, d],
                dst_ref=recv.at[e, pl.ds(pl.multiple_of(ROWS * f, 16), ROWS)],
                send_sem=a2a_s.at[e], recv_sem=a2a_r.at[e],
                device_id=(r, d), device_id_type=MESH,
            ).start()
            return 0

        lax.fori_loop(1, N, body, 0)

    def send_tail():
        def body(o, _):
            d = rem(f + o, N)
            pltpu.make_async_remote_copy(
                src_ref=send_t.at[d], dst_ref=recv_t.at[f],
                send_sem=a2a_s.at[2], recv_sem=a2a_r.at[2],
                device_id=(r, d), device_id_type=MESH,
            ).start()
            return 0

        lax.fori_loop(1, N, body, 0)

    loads[0].wait()
    pack_main(0)
    pl.semaphore_wait(bar, N - 1 + R - 1)
    send_main(0)
    loads[1].wait()
    pack_main(1)
    send_main(1)
    pack_tail()
    send_tail()
    for e in range(2):
        recv[e, pl.ds(pl.multiple_of(ROWS * f, 16), ROWS)] = send[e, f]
    recv_t[f] = send_t[f]

    def idx_copy():
        return pltpu.make_async_remote_copy(
            src_ref=own_idx, dst_ref=idx_all.at[r],
            send_sem=idx_s, recv_sem=idx_r, device_id=(own, f), device_id_type=MESH,
        )

    @pl.when(jnp.logical_not(is_owner))
    def _():
        idx_copy().start()

    loads[2].wait()
    pick = (lax.broadcasted_iota(I32, (SPAN, SPAN), 0) == flat_idx[0:1, :]).astype(F32)
    pick = jnp.transpose(pick).astype(BF16)
    for part in range(2):
        rows = dot(pick, cos_v[part]).astype(BF16)
        for g in range(15):
            low[32 * g + 16 * part:32 * g + 16 * part + 16] = rows[16 * g:16 * g + 16]

    @pl.when(is_owner)
    def _():
        idx_all[r] = own_idx[...]
        pltpu.make_async_copy(idx_all.at[pl.ds(0, R - 1)], idx_all.at[pl.ds(0, R - 1)], idx_r).wait()
        merged = idx_all[0]
        for p in range(1, R):
            merged = jnp.where(lane16 < 16 * p, merged, idx_all[p])
        kk = lax.broadcasted_iota(I32, (SPAN, 128), 0)
        for g in range(15):
            hot = (kk == merged[g:g + 1, :]).astype(F32).astype(BF16)
            basis[g, :, 0:128] = dot(cos_v[2], hot).astype(BF16)
            basis[g, :, 128:256] = dot(cos_v[3], hot).astype(BF16)

    loads[3].wait()

    place16 = rem(lane16 - 32 * fm + 128, 128)
    place128 = rem(lanes((128, 128)) - 32 * fm + 128, 128)

    def turned(e, c):
        return jnp.concatenate(
            [
                e_v[e, pl.ds(pl.multiple_of(32 * rem(i - fm + 4, 4), 32), 32), SPAN * c:SPAN * c + SPAN]
                for i in range(4)
            ],
            axis=0,
        )

    def main_tiles(e):
        pltpu.make_async_copy(
            recv.at[e, pl.ds(0, (N - 1) * ROWS)], recv.at[e, pl.ds(0, (N - 1) * ROWS)], a2a_r.at[e]
        ).wait()
        for c in range(6):
            b = 6 * e + c
            ga, limit = (5 * b) // 4, 128 - 32 * (b % 4)
            x = recv[e, SPAN * c:SPAN * c + SPAN]
            er = turned(e, c)
            rows = low[32 * ga:32 * ga + 64]
            o = dot(rows, x) + 0.95 * dot_nt(rows, er)
            pa, pb = o[0:16] + o[16:32], o[32:48] + o[48:64]
            first = place16 < limit
            ka = jnp.where(first, pa, 0.0).astype(BF16)
            kb = jnp.where(first, 0.0, pb).astype(BF16)
            kept[b] = ka + kb
            back = dot_tn(jnp.concatenate([ka, ka, kb, kb], axis=0), rows)
            en = 0.95 * er.astype(F32) + jnp.transpose(x.astype(F32)) - back
            en = en.astype(BF16)
            for i in range(4):
                err_out[
                    e, pl.ds(pl.multiple_of(32 * rem(i - fm + 4, 4), 32), 32), SPAN * c:SPAN * c + SPAN
                ] = en[32 * i:32 * i + 32]

    def tail_tiles():
        pltpu.make_async_copy(
            recv_t.at[pl.ds(0, N - 1)], recv_t.at[pl.ds(0, N - 1)], a2a_r.at[2]
        ).wait()
        for tb in range(3):
            for t16 in range(16):
                v = None
                for j in range(4):
                    b = 4 * tb + j
                    e, row = b // 6, SPAN * (b % 6) + 16 * t16
                    s, g = row // ROWS, 3 * e + (row % ROWS) // 16
                    w = recv_t[s, 16 * (g // 4):16 * (g // 4) + 16].astype(F32)
                    sh = (32 * (j - g)) % 128
                    w = pltpu.roll(w, sh, 1) if sh else w
                    v = w if v is None else jnp.where(lane16 < 32 * j, v, w)
                x_t[tb, 16 * t16:16 * t16 + 16] = v.astype(BF16)
        for tb in range(3):
            x = x_t[tb]
            er = jnp.concatenate(
                [
                    e_v[(4 * tb + j) // 6, 128:160, SPAN * ((4 * tb + j) % 6):SPAN * ((4 * tb + j) % 6) + SPAN]
                    for j in range(4)
                ],
                axis=0,
            )
            base = 32 * (5 * tb + 1)
            rows = low[base:base + 128]
            o = dot(rows, x) + 0.95 * dot_nt(rows, er)
            ks = []
            total = None
            for j in range(4):
                p = o[32 * j:32 * j + 16] + o[32 * j + 16:32 * j + 32]
                k = jnp.where(lane16 // 32 == j, p, 0.0).astype(BF16)
                ks += [k, k]
                total = k if total is None else total + k
            kept[12 + tb] = total
            back = dot_tn(jnp.concatenate(ks, axis=0), rows)
            en = 0.95 * er.astype(F32) + jnp.transpose(x.astype(F32)) - back
            en = en.astype(BF16)
            for j in range(4):
                e, c = (4 * tb + j) // 6, (4 * tb + j) % 6
                err_out[e, 128:160, SPAN * c:SPAN * c + SPAN] = en[32 * j:32 * j + 32]

    FIRST, COUNT = (0, 6, 12), (6, 6, 3)

    def kept_copy(p):
        tiles = pl.ds(FIRST[p], COUNT[p])
        return pltpu.make_async_remote_copy(
            src_ref=kept.at[tiles],
            dst_ref=kept_all.at[tiles, pl.ds(pl.multiple_of(16 * r, 16), 16)],
            send_sem=kept_s.at[p], recv_sem=kept_r.at[p],
            device_id=(own, f), device_id_type=MESH,
        )

    def send_kept(p):
        @pl.when(jnp.logical_not(is_owner))
        def _():
            kept_copy(p).start()

    def take_kept(p):
        for b in range(FIRST[p], FIRST[p] + COUNT[p]):
            kept_all[b, pl.ds(pl.multiple_of(16 * r, 16), 16)] = kept[b]
        part = kept_all.at[pl.ds(0, COUNT[p]), pl.ds(0, 16 * (R - 1))]
        pltpu.make_async_copy(part, part, kept_r.at[p]).wait()

    def upd_main_copy(e, d):
        return pltpu.make_async_remote_copy(
            src_ref=u_out.at[e, pl.ds(pl.multiple_of(ROWS * d, 16), ROWS)],
            dst_ref=upd.at[e, r, y],
            send_sem=upd_s.at[e], recv_sem=upd_r.at[e],
            device_id=(r, d), device_id_type=MESH,
        )

    def average_main(e):
        @pl.when(is_owner)
        def _():
            take_kept(e)
            for c in range(6):
                b = 6 * e + c
                ga, limit = (5 * b) // 4, 128 - 32 * (b % 4)
                k = kept_all[b]
                if limit == 128:
                    u = dot(basis[ga], jnp.concatenate([k, k], axis=0))
                else:
                    zero = jnp.zeros_like(k)
                    first = place128 < limit
                    ka = jnp.where(first, k, zero)
                    kb = jnp.where(first, zero, k)
                    u = dot(basis[ga], jnp.concatenate([ka, ka], axis=0))
                    u = u + dot(basis[ga + 1], jnp.concatenate([kb, kb], axis=0))
                u_out[e, SPAN * c:SPAN * c + SPAN] = (u * 0.125).astype(BF16)

            def body(o, _):
                upd_main_copy(e, rem(f + o, N)).start()
                return 0

            lax.fori_loop(1, N, body, 0)
            upd[e, r, y] = u_out[e, pl.ds(pl.multiple_of(ROWS * f, 16), ROWS)]

    def average_tail():
        @pl.when(is_owner)
        def _():
            take_kept(2)
            for tb in range(3):
                k = kept_all[12 + tb]
                u = None
                for j in range(4):
                    kj = jnp.where(lanes((128, 128)) // 32 == j, k, jnp.zeros_like(k))
                    v = dot(basis[5 * tb + 1 + j], jnp.concatenate([kj, kj], axis=0))
                    u = v if u is None else u + v
                u_tail[tb] = u * 0.125
            for d in range(N):
                w = [None, None]
                for g in range(6):
                    e, row = g // 3, ROWS * d + 16 * (g % 3)
                    b = 6 * e + row // SPAN
                    v = u_tail[b // 4, row % SPAN:row % SPAN + 16]
                    sh = (32 * (g - b)) % 128
                    v = pltpu.roll(v, sh, 1) if sh else v
                    p = w[g // 4]
                    w[g // 4] = v if p is None else jnp.where(lane16 < 32 * (g % 4), p, v)
                u_msg[d, 0:16] = w[0].astype(BF16)
                u_msg[d, 16:32] = w[1].astype(BF16)

            def body(o, _):
                d = rem(f + o, N)
                pltpu.make_async_remote_copy(
                    src_ref=u_msg.at[d], dst_ref=u_recv.at[y],
                    send_sem=upd_s.at[2], recv_sem=upd_r.at[2],
                    device_id=(r, d), device_id_type=MESH,
                ).start()
                return 0

            lax.fori_loop(1, N, body, 0)
            u_recv[y] = u_msg[f]

    def wait_upd(p):
        def some(count):
            part = upd.at[p, 0, pl.ds(0, count)] if p < 2 else u_recv.at[pl.ds(0, count)]
            pltpu.make_async_copy(part, part, upd_r.at[p]).wait()

        @pl.when(is_owner)
        def _():
            some(3)

        @pl.when(jnp.logical_not(is_owner))
        def _():
            some(4)

    def fwd_copy(p, other):
        ref = upd.at[p, r] if p < 2 else upd_tail.at[r]
        return pltpu.make_async_remote_copy(
            src_ref=ref, dst_ref=ref, send_sem=fwd_s.at[p], recv_sem=fwd_r.at[p],
            device_id=(other, f), device_id_type=MESH,
        )

    def forward(p):
        wait_upd(p)
        if p == 2:
            x, core = div(r, 2), rem(r, 2)
            tails = [jnp.zeros((16, 128), F32) for _ in range(6)]
            for yy in range(4):
                m = rem(x - yy + 4, 4)
                for g in range(6):
                    v = u_recv[yy, 16 * (g // 4):16 * (g // 4) + 16].astype(F32)
                    v = pltpu.roll(v, rem(32 * (m - g % 4) + 128, 128), 1)
                    tails[g] = jnp.where(div(lane16, 32) == m, v, tails[g])
            for g in range(6):
                upd_tail[r, 16 * g:16 * g + 16] = tails[g].astype(BF16)
        for o in range(1, R):
            fwd_copy(p, rem(r + o, R)).start()

    main_tiles(0)
    send_kept(0)
    average_main(0)
    main_tiles(1)
    send_kept(1)
    forward(0)
    average_main(1)
    tail_tiles()
    send_kept(2)
    forward(1)
    average_tail()
    forward(2)

    for p in range(3):
        part = upd.at[p, pl.ds(0, R - 1)] if p < 2 else upd_tail.at[pl.ds(0, R - 1)]
        pltpu.make_async_copy(part, part, fwd_r.at[p]).wait()
        pltpu.make_async_copy(part, part, fwd_s.at[p]).wait()
        part = send.at[p, pl.ds(0, N - 1)] if p < 2 else send_t.at[pl.ds(0, N - 1)]
        pltpu.make_async_copy(part, part, a2a_s.at[p]).wait()

    @pl.when(is_owner)
    def _():
        for p in range(3):
            part = u_out.at[p, pl.ds(0, ROWS * (N - 1))] if p < 2 else u_msg.at[pl.ds(0, N - 1)]
            pltpu.make_async_copy(part, part, upd_s.at[p]).wait()

    @pl.when(jnp.logical_not(is_owner))
    def _():
        idx_copy().wait_send()
        for p in range(3):
            kept_copy(p).wait_send()


def exchange(delta, err, cos, own_idx, flat_idx):
    vmem = pl.BlockSpec(memory_space=pltpu.VMEM)
    hbm = pl.BlockSpec(memory_space=pl.ANY)
    return pl.pallas_call(
        exchange_kernel,
        out_shape=(
            pltpu.VMEM((2, R, 4, ROWS, 128), BF16),
            pltpu.VMEM((R, 2 * ROWS, 128), BF16),
            pltpu.VMEM((2, 160, 1536), BF16),
        ),
        in_specs=[hbm, hbm, hbm, vmem, vmem],
        out_specs=(vmem, vmem, vmem),
        scratch_shapes=[
            pltpu.VMEM((2, ROWS, 5120), BF16),
            pltpu.VMEM((2, 160, 1536), BF16),
            pltpu.VMEM((4, SPAN, SPAN), BF16),
            pltpu.VMEM((2, N, ROWS, 128), BF16),
            pltpu.VMEM((N, 32, 128), BF16),
            pltpu.VMEM((2, N * ROWS, 128), BF16),
            pltpu.VMEM((N, 32, 128), BF16),
            pltpu.VMEM((3, SPAN, 128), BF16),
            pltpu.VMEM((15 * 32, SPAN), BF16),
            pltpu.VMEM((15, SPAN, SPAN), BF16),
            pltpu.VMEM((R, 16, 128), I32),
            pltpu.VMEM((15, 16, 128), BF16),
            pltpu.VMEM((15, 128, 128), BF16),
            pltpu.VMEM((2, N * ROWS, 128), BF16),
            pltpu.VMEM((3, SPAN, 128), F32),
            pltpu.VMEM((N, 32, 128), BF16),
            pltpu.VMEM((4, 32, 128), BF16),
            pltpu.SemaphoreType.DMA((4,)),
            pltpu.SemaphoreType.DMA((3,)),
            pltpu.SemaphoreType.DMA((3,)),
            pltpu.SemaphoreType.DMA,
            pltpu.SemaphoreType.DMA,
            pltpu.SemaphoreType.DMA((3,)),
            pltpu.SemaphoreType.DMA((3,)),
            pltpu.SemaphoreType.DMA((3,)),
            pltpu.SemaphoreType.DMA((3,)),
            pltpu.SemaphoreType.DMA((3,)),
            pltpu.SemaphoreType.DMA((3,)),
        ],
        compiler_params=pltpu.CompilerParams(
            collective_id=0, has_side_effects=True, vmem_limit_bytes=32 << 20
        ),
        name="exchange",
    )(delta, err, cos, own_idx, flat_idx)


def finish_kernel(
    upd, upd_tail, err, theta, momentum,
    theta_out, momentum_out, err_out,
    th, mo, err_sem, th_sem, mo_sem, th_out_sem, mo_out_sem,
):
    moved = pltpu.make_async_copy(err, err_out, err_sem)
    moved.start()

    def piece(q):
        return pl.ds(pl.multiple_of(640 * q, 128), 640)

    def read(q):
        return (
            pltpu.make_async_copy(theta.at[:, :, piece(q)], th.at[:, :, piece(q)], th_sem.at[q]),
            pltpu.make_async_copy(momentum.at[:, :, piece(q)], mo.at[:, :, piece(q)], mo_sem.at[q]),
        )

    def write(q):
        return (
            pltpu.make_async_copy(th.at[:, :, piece(q)], theta_out.at[:, :, piece(q)], th_out_sem.at[q]),
            pltpu.make_async_copy(mo.at[:, :, piece(q)], momentum_out.at[:, :, piece(q)], mo_out_sem.at[q]),
        )

    for q in range(8):
        for c in read(q):
            c.start()
    lane = lanes((ROWS, 128))
    for q in range(8):
        for c in read(q):
            c.wait()
        y, core = q // 2, q % 2
        reps = [2 * ((y + m) % 4) + core for m in range(4)]
        for e in range(2):
            main = [upd[e, reps[m], y].astype(F32) for m in range(4)]
            tail = [upd_tail[reps[m], ROWS * e:ROWS * e + ROWS].astype(F32) for m in range(4)]
            tiles = [
                main[0],
                jnp.where(lane < 32, tail[0], main[1]),
                jnp.where(lane < 32, main[1], jnp.where(lane < 64, tail[1], main[2])),
                jnp.where(lane < 64, main[2], jnp.where(lane < 96, tail[2], main[3])),
                jnp.where(lane < 96, main[3], tail[3]),
            ]
            for k in range(5):
                cols = slice(640 * q + 128 * k, 640 * q + 128 * k + 128)
                m_new = 0.9 * mo[e, :, cols] + tiles[k]
                mo[e, :, cols] = m_new
                th[e, :, cols] = th[e, :, cols] - 0.7 * (tiles[k] + 0.9 * m_new)
        for c in write(q):
            c.start()
    for q in range(8):
        for c in write(q):
            c.wait()
    moved.wait()


def finish(upd, upd_tail, err, theta, momentum):
    vmem = pl.BlockSpec(memory_space=pltpu.VMEM)
    hbm = pl.BlockSpec(memory_space=pl.ANY)
    return pl.pallas_call(
        finish_kernel,
        out_shape=(
            jax.ShapeDtypeStruct(theta.shape, F32),
            jax.ShapeDtypeStruct(theta.shape, F32),
            jax.ShapeDtypeStruct(err.shape, BF16),
        ),
        in_specs=[vmem, vmem, vmem, hbm, hbm],
        out_specs=(hbm, hbm, hbm),
        scratch_shapes=[
            pltpu.VMEM((2, ROWS, 5120), F32),
            pltpu.VMEM((2, ROWS, 5120), F32),
            pltpu.SemaphoreType.DMA,
            pltpu.SemaphoreType.DMA((8,)),
            pltpu.SemaphoreType.DMA((8,)),
            pltpu.SemaphoreType.DMA((8,)),
            pltpu.SemaphoreType.DMA((8,)),
        ],
        compiler_params=pltpu.CompilerParams(vmem_limit_bytes=16 << 20),
        name="finish",
    )(upd, upd_tail, err, theta, momentum)


def shards(delta, error, theta, momentum, block_index, block_count):
    idx, count = block_index[0], block_count[0]
    live = jnp.arange(16, dtype=I32)[None, :] < count[:, None]
    idx = jnp.where(live, idx, -1)
    idx = jnp.pad(idx, ((0, 1), (0, 0)), constant_values=-1)
    own_idx = jnp.tile(idx, (1, R))
    flat_idx = jnp.broadcast_to(idx.reshape(1, SPAN), (8, SPAN))
    cos = jnp.asarray(cosine_parts())
    err = jnp.transpose(error[0], (0, 2, 1))
    upd, upd_tail, err_new = exchange(delta[0], err, cos, own_idx, flat_idx)
    theta_new, momentum_new, err_new = finish(upd, upd_tail, err_new, theta, momentum)
    return theta_new, momentum_new, jnp.transpose(err_new, (0, 2, 1))[None]


def solution(mesh):
    return jax.shard_map(
        shards,
        mesh=mesh,
        in_specs=(
            P("replica", None, "fsdp", None),
            P("replica", None, None, "fsdp"),
            P(None, "fsdp", None),
            P(None, "fsdp", None),
            P("replica", "fsdp", None),
            P("replica", "fsdp"),
        ),
        out_specs=(P(None, "fsdp", None), P(None, "fsdp", None), P("replica", None, None, "fsdp")),
        check_vma=False,
    )
```

```python
import functools

import jax
import jax.numpy as jnp
import numpy as np
from jax import lax
from jax.experimental import pallas as pl
from jax.experimental.pallas import tpu as pltpu
from jax.sharding import PartitionSpec as P

SPAN = 256
N = 32
R = 8
ROWS = 48
MESH = pl.DeviceIdType.MESH
F32 = jnp.float32
BF16 = jnp.bfloat16
I32 = jnp.int32


def cosine_table():
    k = np.arange(SPAN, dtype=np.float64)[:, None]
    t = np.arange(SPAN, dtype=np.float64)[None, :]
    m = np.cos(np.pi * (2.0 * t + 1.0) * k / (2.0 * SPAN))
    return (m * np.where(k == 0, np.sqrt(1.0 / SPAN), np.sqrt(2.0 / SPAN))).astype(np.float32)


def div(a, b):
    return lax.div(a, jnp.int32(b))


def rem(a, b):
    return lax.rem(a, jnp.int32(b))


def turn_of(f):
    y, z = div(f, 8), rem(f, 8)
    return 2 * rem(y + z, 4) + div(z, 4)


PIECES = (
    [(48 * n, 0, 48) for n in range(5)] + [(240, 0, 16)],
    [(0, 16, 32)] + [(32 + 48 * n, 0, 48) for n in range(4)] + [(224, 0, 32)],
    [(0, 32, 16)] + [(16 + 48 * n, 0, 48) for n in range(5)],
)


def dot_nt(a, b):
    return lax.dot_general(a, b, (((1,), (1,)), ((), ())), preferred_element_type=F32)


def dot_tn(a, b):
    return lax.dot_general(a, b, (((0,), (0,)), ((), ())), preferred_element_type=F32)


def dot(a, b):
    return jnp.dot(a, b, preferred_element_type=F32)


def lanes(shape):
    return lax.broadcasted_iota(I32, shape, len(shape) - 1)


def exchange_kernel(
    delta, err, cos, idx, count, theta, momentum,
    upd, upd_tail, err_out, theta_v, momentum_v,
    d_v, e_v, table, cos_v, idx_v, count_s, lists, own_idx, send, send_t, recv, recv_t, x_t, low, basis,
    from_err, idx_all, merged, kept, kept_in, u_out, u_tail, u_msg, u_recv,
    load_sem, a2a_s, a2a_r, idx_s, idx_r, kept_s, kept_r, upd_s, upd_r, fwd_s, fwd_r,
):
    r = lax.axis_index("replica")
    f = lax.axis_index("fsdp")
    y, z = div(f, 8), rem(f, 8)
    fm = rem(f, 4)
    turn = turn_of(f)
    mine_first = rem(r - turn + R, R)
    has_second = mine_first < 4
    block_of = (mine_first, jnp.where(mine_first < 4, mine_first + 8, mine_first), mine_first,
                rem(mine_first, 4) + 8)
    has_block = (mine_first < 6, (mine_first < 4) | (mine_first >= 6), None, has_second)

    loads = [
        pltpu.make_async_copy(delta.at[0], d_v.at[0], load_sem.at[0]),
        pltpu.make_async_copy(delta.at[1], d_v.at[1], load_sem.at[1]),
        pltpu.make_async_copy(cos, table, load_sem.at[2]),
        pltpu.make_async_copy(err, e_v, load_sem.at[3]),
        pltpu.make_async_copy(idx, idx_v, load_sem.at[4]),
        pltpu.make_async_copy(count, count_s, load_sem.at[5]),
        pltpu.make_async_copy(theta, theta_v, load_sem.at[6]),
        pltpu.make_async_copy(momentum, momentum_v, load_sem.at[7]),
    ]
    for c in loads[:6]:
        c.start()

    bar = pltpu.get_barrier_semaphore()

    def greet_row(o, _):
        pl.semaphore_signal(bar, inc=1, device_id=(r, rem(f + o, N)), device_id_type=MESH)
        return 0

    def greet_col(o, _):
        pl.semaphore_signal(bar, inc=1, device_id=(rem(r + o, R), f), device_id_type=MESH)
        return 0

    lax.fori_loop(1, N, greet_row, 0)
    lax.fori_loop(1, R, greet_col, 0)

    lane16 = lanes((16, 128))

    def pack_main(e):
        def body(q, _):
            for i in range(3):
                rows = pl.ds(16 * i, 16)
                t = [
                    d_v[e, rows, pl.ds(pl.multiple_of(640 * q + 128 * k, 128), 128)]
                    for k in range(5)
                ]
                send[e, 4 * q, rows] = t[0]
                send[e, 4 * q + 1, rows] = jnp.where(lane16 >= 32, t[1], t[2])
                send[e, 4 * q + 2, rows] = jnp.where(lane16 >= 64, t[2], t[3])
                send[e, 4 * q + 3, rows] = jnp.where(lane16 >= 96, t[3], t[4])
            return 0

        lax.fori_loop(0, 8, body, 0)

    def pack_tail():
        def body(q, _):
            zs = []
            for g in range(6):
                e, i = g // 3, g % 3
                t = [
                    d_v[e, 16 * i:16 * i + 16, pl.ds(pl.multiple_of(640 * q + 128 * k, 128), 128)]
                    for k in range(1, 5)
                ]
                v = jnp.where(
                    lane16 < 32, t[0], jnp.where(lane16 < 64, t[1], jnp.where(lane16 < 96, t[2], t[3]))
                )
                zs.append(v.astype(F32))
            for m in range(4):
                w = [None, None]
                for g in range(6):
                    k = g % 4
                    s = (32 * (k - m)) % 128
                    v = pltpu.roll(zs[g], s, 1) if s else zs[g]
                    p = w[g // 4]
                    w[g // 4] = v if p is None else jnp.where(lane16 < 32 * k, p, v)
                send_t[4 * q + m, 0:16] = w[0].astype(BF16)
                send_t[4 * q + m, 16:32] = w[1].astype(BF16)
            return 0

        lax.fori_loop(0, 8, body, 0)

    def offsets(half, dy):
        turns = ((1, -1, 2, -2), (3, -3, 4, 0))[half]
        return [(dy, dz) for dz in turns if dy or dz]

    def group_ref(j):
        n = len(offsets(j % 2, j % 8 // 2))
        return send.at[j // 8, pl.ds(0, n)] if j < 16 else send_t.at[pl.ds(0, n)]

    def group_start(j):
        p = j // 8
        for dy, dz in offsets(j % 2, j % 8 // 2):
            d = 8 * rem(y + dy, 4) + rem(z + dz + 8, 8)
            if p < 2:
                src, dst = send.at[p, d], recv.at[p, pl.ds(pl.multiple_of(ROWS * f, 16), ROWS)]
            else:
                src, dst = send_t.at[d], recv_t.at[f]
            pltpu.make_async_remote_copy(
                src_ref=src, dst_ref=dst, send_sem=a2a_s.at[j], recv_sem=a2a_r.at[p],
                device_id=(r, d), device_id_type=MESH,
            ).start()

    def group_wait(j):
        pltpu.make_async_copy(group_ref(j), group_ref(j), a2a_s.at[j]).wait()

    started = [0]

    def pump(upto):
        for j in range(started[0], upto):
            group_start(j)
        started[0] = max(started[0], upto)

    loads[0].wait()
    pack_main(0)
    pl.semaphore_wait(bar, N - 1 + R - 1)
    pump(8)
    loads[1].wait()
    pack_main(1)
    for c in loads[6:]:
        c.start()
    pump(16)
    pack_tail()
    for e in range(2):
        recv[e, pl.ds(pl.multiple_of(ROWS * f, 16), ROWS)] = send[e, f]
    recv_t[f] = send_t[f]

    loads[4].wait()
    loads[5].wait()
    lists[...] = jnp.full((16, 128), -1.0, F32)
    for g in range(15):
        named = jnp.where(lanes((1, 16)) < count_s[0, g], idx_v[g], -1)
        lists[g:g + 1, 0:16] = named.astype(F32)
    held = lists[...].astype(BF16)
    into, outof = lax.broadcasted_iota(I32, (128, 128), 0), lanes((128, 128))
    spread = jnp.where((into < 16) & (rem(outof, 16) == into), 1.0, 0.0).astype(BF16)
    own_idx[...] = dot(held, spread)

    idx_all[r] = own_idx[...]
    for o in range(1, R):
        pltpu.make_async_remote_copy(
            src_ref=own_idx, dst_ref=idx_all.at[r],
            send_sem=idx_s, recv_sem=idx_r, device_id=(rem(r + o, R), f), device_id_type=MESH,
        ).start()

    loads[2].wait()
    for way, full in enumerate((table[...], jnp.transpose(table[...]))):
        high = full.astype(BF16)
        cos_v[2 * way] = high
        cos_v[2 * way + 1] = (full - high.astype(F32)).astype(BF16)
    slot, group = lax.broadcasted_iota(I32, (SPAN, 16), 0), lanes((SPAN, 16))
    mine = dot(jnp.where(div(slot, 16) == group, 1.0, 0.0).astype(BF16), held)
    slot, lane = lax.broadcasted_iota(I32, (SPAN, 128), 0), lanes((SPAN, 128))
    mine = jnp.where(rem(slot, 16) == lane, mine, 0.0).astype(BF16)
    mine = dot(mine, jnp.ones((128, SPAN), BF16))
    pick = jnp.where(mine == lanes((SPAN, SPAN)).astype(F32), 1.0, 0.0).astype(BF16)
    for part in range(2):
        rows = dot(pick, cos_v[part]).astype(BF16)
        for g in range(15):
            low[32 * g + 16 * part:32 * g + 16 * part + 16] = rows[16 * g:16 * g + 16]

    part = idx_all.at[pl.ds(0, R - 1)]
    pltpu.make_async_copy(part, part, idx_r).wait()
    lists_all = idx_all[0]
    for p in range(1, R):
        lists_all = jnp.where(lane16 < 16 * p, lists_all, idx_all[p])
    merged[...] = lists_all
    kk = lax.broadcasted_iota(I32, (SPAN, 128), 0).astype(F32)
    first_a, first_b = div(5 * block_of[0], 4), div(5 * block_of[1], 4)
    first_a = jnp.minimum(first_a, 13)
    tails = [b + 1 + div(b, 4) for b in (mine_first, rem(mine_first, 4) + 8)]
    for s, g in enumerate((first_a, first_a + 1, first_b, first_b + 1, tails[0], tails[1])):
        hot = jnp.where(kk == merged[pl.ds(g, 1), :], 1.0, 0.0).astype(BF16)
        basis[s, :, 0:128] = dot(cos_v[2], hot).astype(BF16)
        basis[s, :, 128:256] = dot(cos_v[3], hot).astype(BF16)

    loads[3].wait()

    place16 = rem(lane16 - 32 * fm + 128, 128)
    place128 = rem(lanes((128, 128)) - 32 * fm + 128, 128)

    def turned(e, c):
        return jnp.concatenate(
            [
                e_v[e, pl.ds(pl.multiple_of(32 * rem(i - fm + 4, 4), 32), 32), SPAN * c:SPAN * c + SPAN]
                for i in range(4)
            ],
            axis=0,
        )

    def err_columns(tb):
        return jnp.concatenate(
            [
                e_v[(4 * tb + j) // 6, 128:160, SPAN * ((4 * tb + j) % 6):SPAN * ((4 * tb + j) % 6) + SPAN]
                for j in range(4)
            ],
            axis=0,
        )

    def main_rows(b):
        ga = (5 * b) // 4
        return low[32 * ga:32 * ga + 64]

    def tail_rows(tb):
        base = 32 * (5 * tb + 1)
        return low[base:base + 128]

    def main_select(b, o):
        pa, pb = o[0:16] + o[16:32], o[32:48] + o[48:64]
        return jnp.where(place16 < 128 - 32 * (b % 4), pa, pb)

    def tail_select(o):
        p = o[0:16] + o[16:32]
        for j in range(1, 4):
            p = jnp.where(lane16 < 32 * j, p, o[32 * j:32 * j + 16] + o[32 * j + 16:32 * j + 32])
        return p

    for b in range(12):
        from_err[b] = 0.95 * main_select(b, dot_nt(main_rows(b), turned(b // 6, b % 6)))
    for tb in range(3):
        from_err[12 + tb] = 0.95 * tail_select(dot_nt(tail_rows(tb), err_columns(tb)))

    def take_delta(p):
        part = recv.at[p, pl.ds(0, (N - 1) * ROWS)] if p < 2 else recv_t.at[pl.ds(0, N - 1)]
        pltpu.make_async_copy(part, part, a2a_r.at[p]).wait()

    def pick_main(e):
        take_delta(e)
        for c in range(6):
            b = 6 * e + c
            x = recv[e, SPAN * c:SPAN * c + SPAN]
            kept[b] = (main_select(b, dot(main_rows(b), x)) + from_err[b]).astype(BF16)

    def pick_tail():
        take_delta(2)
        for tb in range(3):
            for t16 in range(16):
                v = None
                for j in range(4):
                    b = 4 * tb + j
                    e, row = b // 6, SPAN * (b % 6) + 16 * t16
                    s, g = row // ROWS, 3 * e + (row % ROWS) // 16
                    w = recv_t[s, 16 * (g // 4):16 * (g // 4) + 16].astype(F32)
                    sh = (32 * (j - g)) % 128
                    w = pltpu.roll(w, sh, 1) if sh else w
                    v = w if v is None else jnp.where(lane16 < 32 * j, v, w)
                x_t[tb, 16 * t16:16 * t16 + 16] = v.astype(BF16)
            kept[12 + tb] = (tail_select(dot(tail_rows(tb), x_t[tb])) + from_err[12 + tb]).astype(BF16)

    def tile_of(slot, b8):
        if slot == 0:
            return jnp.minimum(b8, 5)
        if slot == 1:
            return jnp.where(b8 < 4, b8 + 8, jnp.maximum(b8, 6))
        return 12 + div(b8, 4) if slot == 2 else 14

    def send_kept(slot):
        rows = pl.ds(pl.multiple_of(16 * r, 16), 16)
        for o in range(1, R):
            pltpu.make_async_remote_copy(
                src_ref=kept.at[tile_of(slot, rem(mine_first + o, R))], dst_ref=kept_in.at[slot, rows],
                send_sem=kept_s.at[slot], recv_sem=kept_r.at[slot],
                device_id=(rem(r + o, R), f), device_id_type=MESH,
            ).start()
        pltpu.make_async_copy(
            kept.at[tile_of(slot, mine_first)], kept_in.at[slot, rows], kept_r.at[slot]
        ).start()

    def restore_main(e):
        for c in range(6):
            b = 6 * e + c
            k, zero = kept[b], jnp.zeros((16, 128), BF16)
            first = place16 < 128 - 32 * (b % 4)
            ka, kb = jnp.where(first, k, zero), jnp.where(first, zero, k)
            back = dot_tn(jnp.concatenate([ka, ka, kb, kb], axis=0), main_rows(b))
            x = recv[e, SPAN * c:SPAN * c + SPAN].astype(F32)
            en = (0.95 * turned(e, c).astype(F32) + jnp.transpose(x) - back).astype(BF16)
            for i in range(4):
                err_out[
                    e, pl.ds(pl.multiple_of(32 * rem(i - fm + 4, 4), 32), 32), SPAN * c:SPAN * c + SPAN
                ] = en[32 * i:32 * i + 32]

    def restore_tail():
        for tb in range(3):
            k, zero = kept[12 + tb], jnp.zeros((16, 128), BF16)
            ks = []
            for j in range(4):
                kj = jnp.where((lane16 >= 32 * j) & (lane16 < 32 * j + 32), k, zero)
                ks += [kj, kj]
            back = dot_tn(jnp.concatenate(ks, axis=0), tail_rows(tb))
            en = 0.95 * err_columns(tb).astype(F32) + jnp.transpose(x_t[tb].astype(F32)) - back
            en = en.astype(BF16)
            for j in range(4):
                e, c = (4 * tb + j) // 6, (4 * tb + j) % 6
                err_out[e, 128:160, SPAN * c:SPAN * c + SPAN] = en[32 * j:32 * j + 32]

    def when(flag, body):
        if flag is None:
            body()
        else:
            pl.when(flag)(body)

    def upd_move(s, v, n, what):
        b = block_of[s]
        e, c = div(b, 6), rem(b, 6)
        at, to, rows = PIECES[v][n]
        d = 16 * div(c, 3) + 5 * v + n
        if s < 2:
            src, dst = u_out.at[s, pl.ds(at, rows)], upd.at[s, r, y, pl.ds(to, rows)]
        else:
            src, dst = u_msg.at[s - 2, n], u_recv.at[1 if to else 0, e, y]
        arrived = upd_r.at[min(s, 2)]

        @pl.when(d != f)
        def _():
            m = pltpu.make_async_remote_copy(
                src_ref=src, dst_ref=dst, send_sem=upd_s.at[s, n], recv_sem=arrived,
                device_id=(r, d), device_id_type=MESH,
            )
            m.start() if what == "start" else m.wait_send()

        if what == "start":
            @pl.when(d == f)
            def _():
                pltpu.make_async_copy(src, dst, arrived).start()

    def upd_all(s, what):
        for v in range(3):
            @pl.when(rem(rem(block_of[s], 6), 3) == v)
            def _():
                for n in range(6):
                    upd_move(s, v, n, what)

    def take_kept(s):
        pltpu.make_async_copy(kept_in.at[s], kept_in.at[s], kept_r.at[s]).wait()
        return kept_in[s]

    def average_main(s):
        k = take_kept(s)
        zero = jnp.zeros_like(k)
        first = place128 < 128 - 32 * rem(block_of[s], 4)
        ka = jnp.where(first, k, zero)
        kb = jnp.where(first, zero, k)
        u = dot(basis[2 * s], jnp.concatenate([ka, ka], axis=0))
        u = u + dot(basis[2 * s + 1], jnp.concatenate([kb, kb], axis=0))
        u_out[s] = (u * 0.125).astype(BF16)
        when(has_block[s], functools.partial(upd_all, s, "start"))

    def average_tail():
        into, outof = lax.broadcasted_iota(I32, (128, 128), 0), lanes((128, 128))
        same = (div(into, 32) == rem(mine_first, 4)) & (rem(into, 32) == rem(outof, 32))
        same = jnp.where(same, 1.0, 0.0).astype(BF16)
        ks = [dot(take_kept(s), same).astype(BF16) for s in (2, 3)]
        for s in (2, 3):
            k = ks[s - 2]
            u_tail[s - 2] = dot(basis[2 + s], jnp.concatenate([k, k], axis=0)) * 0.125
        for s in (2, 3):
            for v in range(3):
                @pl.when(rem(rem(block_of[s], 6), 3) == v)
                def _():
                    for n, (at, to, rows) in enumerate(PIECES[v]):
                        w = None
                        for i in range(rows // 16):
                            x = u_tail[s - 2, at + 16 * i:at + 16 * i + 16]
                            w = x if w is None else jnp.where(lane16 < to * 2 + 32 * i, w, x)
                        u_msg[s - 2, n] = w.astype(BF16)
            when(has_block[s], functools.partial(upd_all, s, "start"))

    chunk = [div(3 * f + i, 16) for i in range(3)]

    def wait_upd(p):
        def some(part):
            pltpu.make_async_copy(part, part, upd_r.at[p]).wait()

        if p < 2:
            some(upd.at[p, 0])
            return

        @pl.when(chunk[0] == chunk[2])
        def _():
            some(u_recv.at[0])

        @pl.when(chunk[0] != chunk[2])
        def _():
            some(u_recv)

    def fwd_copy(p, other):
        ref = upd.at[p, r] if p < 2 else upd_tail.at[r]
        return pltpu.make_async_remote_copy(
            src_ref=ref, dst_ref=ref, send_sem=fwd_s.at[p], recv_sem=fwd_r.at[p],
            device_id=(other, f), device_id_type=MESH,
        )

    def forward(p):
        wait_upd(p)
        if p == 2:
            for e in range(2):
                for i in range(3):
                    whole = jnp.zeros((16, 128), F32)
                    behind = div(rem(r - 6 * e - chunk[i] + 2 * R, R), 2)
                    for yy in range(4):
                        m = rem(behind - yy + 4, 4)
                        v = u_recv[chunk[i] - chunk[0], e, yy].astype(F32)
                        v = pltpu.roll(v, rem(32 * (m - i) + 128, 128), 1)
                        whole = jnp.where(div(lane16, 32) == m, v, whole)
                    upd_tail[r, ROWS * e + 16 * i:ROWS * e + 16 * i + 16] = whole.astype(BF16)
        for o in range(1, R):
            fwd_copy(p, rem(r + o, R)).start()

    pick_main(0)
    send_kept(0)
    restore_main(0)
    pump(20)
    average_main(0)
    pump(24)
    pick_main(1)
    send_kept(1)
    forward(0)
    restore_main(1)
    average_main(1)
    pick_tail()
    send_kept(2)
    send_kept(3)
    average_tail()
    forward(1)
    restore_tail()
    forward(2)

    for p in range(3):
        part = upd.at[p, pl.ds(0, R - 1)] if p < 2 else upd_tail.at[pl.ds(0, R - 1)]
        pltpu.make_async_copy(part, part, fwd_r.at[p]).wait()
        pltpu.make_async_copy(part, part, fwd_s.at[p]).wait()

    for j in range(24):
        group_wait(j)
    for c in loads[6:]:
        c.wait()

    part = idx_all.at[pl.ds(0, R - 1)]
    pltpu.make_async_copy(part, part, idx_s).wait()
    for s in range(4):
        pltpu.make_async_copy(
            kept_in.at[s, pl.ds(0, 16 * (R - 1))], kept_in.at[s, pl.ds(0, 16 * (R - 1))], kept_s.at[s]
        ).wait()
    for s in range(4):
        when(has_block[s], functools.partial(upd_all, s, "wait"))


def exchange(delta, err, cos, idx, count, theta, momentum):
    vmem = pl.BlockSpec(memory_space=pltpu.VMEM)
    hbm = pl.BlockSpec(memory_space=pltpu.HBM)
    args = (delta, err, cos, idx, count, theta, momentum)
    args = [pltpu.with_memory_space_constraint(a, pltpu.HBM) for a in args]
    return pl.pallas_call(
        exchange_kernel,
        out_shape=(
            pltpu.VMEM((2, R, 4, ROWS, 128), BF16),
            pltpu.VMEM((R, 2 * ROWS, 128), BF16),
            pltpu.VMEM((2, 160, 1536), BF16),
            pltpu.VMEM(theta.shape, F32),
            pltpu.VMEM(theta.shape, F32),
        ),
        in_specs=[hbm] * 7,
        out_specs=(vmem,) * 5,
        scratch_shapes=[
            pltpu.VMEM((2, ROWS, 5120), BF16),
            pltpu.VMEM((2, 160, 1536), BF16),
            pltpu.VMEM((SPAN, SPAN), F32),
            pltpu.VMEM((4, SPAN, SPAN), BF16),
            pltpu.VMEM((15, 1, 16), I32),
            pltpu.SMEM((1, 15), I32),
            pltpu.VMEM((16, 128), F32),
            pltpu.VMEM((16, 128), F32),
            pltpu.VMEM((2, N, ROWS, 128), BF16),
            pltpu.VMEM((N, 32, 128), BF16),
            pltpu.VMEM((2, N * ROWS, 128), BF16),
            pltpu.VMEM((N, 32, 128), BF16),
            pltpu.VMEM((3, SPAN, 128), BF16),
            pltpu.VMEM((15 * 32, SPAN), BF16),
            pltpu.VMEM((6, SPAN, SPAN), BF16),
            pltpu.VMEM((15, 16, 128), F32),
            pltpu.VMEM((R, 16, 128), F32),
            pltpu.VMEM((16, 128), F32),
            pltpu.VMEM((15, 16, 128), BF16),
            pltpu.VMEM((4, 128, 128), BF16),
            pltpu.VMEM((2, SPAN, 128), BF16),
            pltpu.VMEM((2, SPAN, 128), F32),
            pltpu.VMEM((2, 6, 16, 128), BF16),
            pltpu.VMEM((2, 2, 4, 16, 128), BF16),
            pltpu.SemaphoreType.DMA((8,)),
            pltpu.SemaphoreType.DMA((24,)),
            pltpu.SemaphoreType.DMA((3,)),
            pltpu.SemaphoreType.DMA,
            pltpu.SemaphoreType.DMA,
            pltpu.SemaphoreType.DMA((4,)),
            pltpu.SemaphoreType.DMA((4,)),
            pltpu.SemaphoreType.DMA((4, 6)),
            pltpu.SemaphoreType.DMA((3,)),
            pltpu.SemaphoreType.DMA((3,)),
            pltpu.SemaphoreType.DMA((3,)),
        ],
        compiler_params=pltpu.CompilerParams(
            collective_id=0, has_side_effects=True, vmem_limit_bytes=32 << 20
        ),
        name="exchange",
    )(*args)


def finish_kernel(
    upd, upd_tail, err, theta, momentum,
    theta_out, momentum_out, err_out,
    th, mo, err_sem, th_sem, mo_sem,
):
    moved = pltpu.make_async_copy(err, err_out, err_sem)
    moved.start()

    def write(q):
        cols = pl.ds(640 * q, 640)
        return (
            pltpu.make_async_copy(th.at[:, :, cols], theta_out.at[:, :, cols], th_sem.at[q]),
            pltpu.make_async_copy(mo.at[:, :, cols], momentum_out.at[:, :, cols], mo_sem.at[q]),
        )

    f = lax.axis_index("fsdp")
    lane = lanes((16, 128))
    for q in range(8):
        y, core = q // 2, q % 2
        for e in range(2):
            for i in range(3):
                rows = slice(16 * i, 16 * i + 16)
                shift = 6 * e + div(3 * f + i, 16) + core
                reps = [rem(shift + 2 * ((y + m) % 4), R) for m in range(4)]
                main = [upd[e, reps[m], y, rows].astype(F32) for m in range(4)]
                tail = [
                    upd_tail[reps[m], ROWS * e + 16 * i:ROWS * e + 16 * i + 16].astype(F32)
                    for m in range(4)
                ]
                tiles = [
                    main[0],
                    jnp.where(lane < 32, tail[0], main[1]),
                    jnp.where(lane < 32, main[1], jnp.where(lane < 64, tail[1], main[2])),
                    jnp.where(lane < 64, main[2], jnp.where(lane < 96, tail[2], main[3])),
                    jnp.where(lane < 96, main[3], tail[3]),
                ]
                for k in range(5):
                    cols = slice(640 * q + 128 * k, 640 * q + 128 * k + 128)
                    m_new = 0.9 * momentum[e, rows, cols] + tiles[k]
                    mo[e, rows, cols] = m_new
                    th[e, rows, cols] = theta[e, rows, cols] - 0.7 * (tiles[k] + 0.9 * m_new)
        for c in write(q):
            c.start()
    for q in range(8):
        for c in write(q):
            c.wait()
    moved.wait()


def finish(*args):
    vmem = pl.BlockSpec(memory_space=pltpu.VMEM)
    hbm = pl.BlockSpec(memory_space=pltpu.HBM)
    upd, upd_tail, err, theta, momentum = args
    args = [pltpu.with_memory_space_constraint(a, pltpu.VMEM) for a in args]
    return pl.pallas_call(
        finish_kernel,
        out_shape=(
            jax.ShapeDtypeStruct(theta.shape, F32),
            jax.ShapeDtypeStruct(theta.shape, F32),
            jax.ShapeDtypeStruct(err.shape, BF16),
        ),
        in_specs=[vmem] * 5,
        out_specs=(hbm, hbm, hbm),
        scratch_shapes=[
            pltpu.VMEM((2, ROWS, 5120), F32),
            pltpu.VMEM((2, ROWS, 5120), F32),
            pltpu.SemaphoreType.DMA,
            pltpu.SemaphoreType.DMA((8,)),
            pltpu.SemaphoreType.DMA((8,)),
        ],
        compiler_params=pltpu.CompilerParams(vmem_limit_bytes=16 << 20),
        name="finish",
    )(*args)


def shards(delta, error, theta, momentum, block_index, block_count):
    cos = jnp.asarray(cosine_table())
    err = jnp.transpose(error[0], (0, 2, 1))
    idx = block_index.reshape(15, 1, 16)
    made = exchange(delta[0], err, cos, idx, block_count, theta, momentum)
    theta_new, momentum_new, err_new = finish(*made)
    return theta_new, momentum_new, jnp.transpose(err_new, (0, 2, 1))[None]


def solution(mesh):
    return jax.shard_map(
        shards,
        mesh=mesh,
        in_specs=(
            P("replica", None, "fsdp", None),
            P("replica", None, None, "fsdp"),
            P(None, "fsdp", None),
            P(None, "fsdp", None),
            P("replica", "fsdp", None),
            P("replica", "fsdp"),
        ),
        out_specs=(P(None, "fsdp", None), P(None, "fsdp", None), P("replica", None, None, "fsdp")),
        check_vma=False,
    )
```

```python
import functools

import jax
import jax.numpy as jnp
import numpy as np
from jax import lax
from jax.experimental import pallas as pl
from jax.experimental.pallas import tpu as pltpu
from jax.sharding import PartitionSpec as P

SPAN = 256
N = 32
R = 8
ROWS = 48
MESH = pl.DeviceIdType.MESH
F32 = jnp.float32
BF16 = jnp.bfloat16
I32 = jnp.int32


def cosine_table():
    k = np.arange(SPAN, dtype=np.float64)[:, None]
    t = np.arange(SPAN, dtype=np.float64)[None, :]
    m = np.cos(np.pi * (2.0 * t + 1.0) * k / (2.0 * SPAN))
    return (m * np.where(k == 0, np.sqrt(1.0 / SPAN), np.sqrt(2.0 / SPAN))).astype(np.float32)


def div(a, b):
    return lax.div(a, jnp.int32(b))


def rem(a, b):
    return lax.rem(a, jnp.int32(b))


def turn_of(f):
    y, z = div(f, 8), rem(f, 8)
    return 2 * rem(y + z, 4) + div(z, 4)


PIECES = (
    [(48 * n, 0, 48) for n in range(5)] + [(240, 0, 16)],
    [(0, 16, 32)] + [(32 + 48 * n, 0, 48) for n in range(4)] + [(224, 0, 32)],
    [(0, 32, 16)] + [(16 + 48 * n, 0, 48) for n in range(5)],
)


def dot_nt(a, b):
    return lax.dot_general(a, b, (((1,), (1,)), ((), ())), preferred_element_type=F32)


def dot_tn(a, b):
    return lax.dot_general(a, b, (((0,), (0,)), ((), ())), preferred_element_type=F32)


def dot(a, b):
    return jnp.dot(a, b, preferred_element_type=F32)


def lanes(shape):
    return lax.broadcasted_iota(I32, shape, len(shape) - 1)


def exchange_kernel(
    delta, err, cos, idx, count, theta, momentum,
    upd, upd_tail, last_tail, err_out, theta_v, momentum_v,
    d_v, e_v, table, cos_v, idx_v, count_s, lists, own_idx, send, send_t, recv, recv_t, x_t, low, basis,
    from_err, idx_all, merged, kept, kept_in, u_out, u_tail, u_msg, u_recv,
    kept_last, basis_last, u_last, last_msg, last_recv,
    load_sem, a2a_s, a2a_r, idx_s, idx_r, kept_s, kept_r, upd_s, upd_r, fwd_s, fwd_r, last_s, last_r,
):
    r = lax.axis_index("replica")
    f = lax.axis_index("fsdp")
    y, z = div(f, 8), rem(f, 8)
    fm = rem(f, 4)
    turn = turn_of(f)
    mine_first = rem(r - turn + R, R)
    block_of = (mine_first, jnp.where(mine_first < 4, mine_first + 8, mine_first))
    has_block = (mine_first < 6, (mine_first < 4) | (mine_first >= 6))

    loads = [
        pltpu.make_async_copy(delta.at[0], d_v.at[0], load_sem.at[0]),
        pltpu.make_async_copy(delta.at[1], d_v.at[1], load_sem.at[1]),
        pltpu.make_async_copy(cos, table, load_sem.at[2]),
        pltpu.make_async_copy(err, e_v, load_sem.at[3]),
        pltpu.make_async_copy(idx, idx_v, load_sem.at[4]),
        pltpu.make_async_copy(count, count_s, load_sem.at[5]),
        pltpu.make_async_copy(theta, theta_v, load_sem.at[6]),
        pltpu.make_async_copy(momentum, momentum_v, load_sem.at[7]),
    ]
    loads[0].start()

    bar = pltpu.get_barrier_semaphore()

    for dy in (2, 1, 3, 0):
        for dz in (4, 3, -3, 2, -2, 1, -1, 0):
            if dy or dz:
                d = 8 * rem(y + dy, 4) + rem(z + dz + 8, 8)
                pl.semaphore_signal(bar, inc=1, device_id=(r, d), device_id_type=MESH)
    for o in (4, 3, 5, 2, 6, 1, 7):
        pl.semaphore_signal(bar, inc=1, device_id=(rem(r + o, R), f), device_id_type=MESH)
    for c in loads[1:6]:
        c.start()

    lane16 = lanes((16, 128))

    def pack_main(e):
        def body(q, _):
            for i in range(3):
                rows = pl.ds(16 * i, 16)
                t = [
                    d_v[e, rows, pl.ds(pl.multiple_of(640 * q + 128 * k, 128), 128)]
                    for k in range(5)
                ]
                send[e, 4 * q, rows] = t[0]
                send[e, 4 * q + 1, rows] = jnp.where(lane16 >= 32, t[1], t[2])
                send[e, 4 * q + 2, rows] = jnp.where(lane16 >= 64, t[2], t[3])
                send[e, 4 * q + 3, rows] = jnp.where(lane16 >= 96, t[3], t[4])
            return 0

        lax.fori_loop(0, 8, body, 0)

    def pack_tail(e):
        def body(q, _):
            zs = []
            for i in range(3):
                t = [
                    d_v[e, 16 * i:16 * i + 16, pl.ds(pl.multiple_of(640 * q + 128 * k, 128), 128)]
                    for k in range(1, 5)
                ]
                v = jnp.where(
                    lane16 < 32, t[0], jnp.where(lane16 < 64, t[1], jnp.where(lane16 < 96, t[2], t[3]))
                )
                zs.append(v.astype(F32))
            for m in range(4):
                w = None
                for i in range(3):
                    s = (32 * (i - m)) % 128
                    v = pltpu.roll(zs[i], s, 1) if s else zs[i]
                    w = v if w is None else jnp.where(lane16 < 32 * i, w, v)
                send_t[e, 4 * q + m] = w.astype(BF16)
            return 0

        lax.fori_loop(0, 8, body, 0)

    def offsets(half, dy):
        turns = ((3, -3, 4, -2), (2, 1, -1, 0))[half]
        return [((2, 1, 3, 0)[dy], dz) for dz in turns if (2, 1, 3, 0)[dy] or dz]

    def group_ref(j):
        n = len(offsets(j % 2, j % 8 // 2))
        return send.at[0, pl.ds(0, n)] if j < 16 else send_t.at[0, pl.ds(0, n)]

    def group_start(j):
        p = j // 8
        for dy, dz in offsets(j % 2, j % 8 // 2):
            d = 8 * rem(y + dy, 4) + rem(z + dz + 8, 8)
            if p < 2:
                src, dst = send.at[p, d], recv.at[p, pl.ds(pl.multiple_of(ROWS * f, 16), ROWS)]
            else:
                src, dst = send_t.at[p - 2, d], recv_t.at[p - 2, f]
            pltpu.make_async_remote_copy(
                src_ref=src, dst_ref=dst, send_sem=a2a_s.at[j], recv_sem=a2a_r.at[p],
                device_id=(r, d), device_id_type=MESH,
            ).start()

    def group_wait(j):
        pltpu.make_async_copy(group_ref(j), group_ref(j), a2a_s.at[j]).wait()

    def groups_start(p, first, last):
        for j in range(8 * p + first, 8 * p + last):
            group_start(j)

    loads[0].wait()
    pack_main(0)
    pl.semaphore_wait(bar, N - 1 + R - 1)
    groups_start(0, 0, 8)
    pack_tail(0)
    groups_start(2, 0, 8)
    loads[1].wait()
    pack_main(1)
    groups_start(1, 0, 8)
    pack_tail(1)
    for c in loads[6:]:
        c.start()
    for e in range(2):
        recv[e, pl.ds(pl.multiple_of(ROWS * f, 16), ROWS)] = send[e, f]
        recv_t[e, f] = send_t[e, f]

    loads[4].wait()
    loads[5].wait()
    lists[...] = jnp.full((16, 128), -1.0, F32)
    for g in range(15):
        named = jnp.where(lanes((1, 16)) < count_s[0, g], idx_v[g], -1)
        lists[g:g + 1, 0:16] = named.astype(F32)
    held = lists[...].astype(BF16)
    into, outof = lax.broadcasted_iota(I32, (128, 128), 0), lanes((128, 128))
    spread = jnp.where((into < 16) & (rem(outof, 16) == into), 1.0, 0.0).astype(BF16)
    own_idx[...] = dot(held, spread)

    idx_all[r] = own_idx[...]
    for o in range(1, R):
        pltpu.make_async_remote_copy(
            src_ref=own_idx, dst_ref=idx_all.at[r],
            send_sem=idx_s, recv_sem=idx_r, device_id=(rem(r + o, R), f), device_id_type=MESH,
        ).start()

    loads[2].wait()
    for way, full in enumerate((table[...], jnp.transpose(table[...]))):
        high = full.astype(BF16)
        cos_v[2 * way] = high
        cos_v[2 * way + 1] = (full - high.astype(F32)).astype(BF16)
    slot, group = lax.broadcasted_iota(I32, (SPAN, 16), 0), lanes((SPAN, 16))
    mine = dot(jnp.where(div(slot, 16) == group, 1.0, 0.0).astype(BF16), held)
    slot, lane = lax.broadcasted_iota(I32, (SPAN, 128), 0), lanes((SPAN, 128))
    mine = jnp.where(rem(slot, 16) == lane, mine, 0.0).astype(BF16)
    mine = dot(mine, jnp.ones((128, SPAN), BF16))
    pick = jnp.where(mine == lanes((SPAN, SPAN)).astype(F32), 1.0, 0.0).astype(BF16)
    for part in range(2):
        rows = dot(pick, cos_v[part]).astype(BF16)
        for g in range(15):
            low[32 * g + 16 * part:32 * g + 16 * part + 16] = rows[16 * g:16 * g + 16]

    part = idx_all.at[pl.ds(0, R - 1)]
    pltpu.make_async_copy(part, part, idx_r).wait()
    lists_all = idx_all[0]
    for p in range(1, R):
        lists_all = jnp.where(lane16 < 16 * p, lists_all, idx_all[p])
    merged[...] = lists_all
    kk = lax.broadcasted_iota(I32, (SPAN, 128), 0).astype(F32)
    first_a, first_b = div(5 * block_of[0], 4), div(5 * block_of[1], 4)
    first_a = jnp.minimum(first_a, 13)
    tail_a = block_of[0] + 1 + div(block_of[0], 4)
    def fill(to, g):
        hot = jnp.where(kk == merged[pl.ds(g, 1), :], 1.0, 0.0).astype(BF16)
        to[:, 0:128] = dot(cos_v[2], hot).astype(BF16)
        to[:, 128:256] = dot(cos_v[3], hot).astype(BF16)

    for s, g in enumerate((first_a, first_a + 1, first_b, first_b + 1, tail_a)):
        fill(basis.at[s], g)
    for c in range(6):
        fill(basis_last.at[c], c + 7 + (c + 6) // 4)

    loads[3].wait()

    place16 = rem(lane16 - 32 * fm + 128, 128)
    place128 = rem(lanes((128, 128)) - 32 * fm + 128, 128)

    def turned(e, c):
        return jnp.concatenate(
            [
                e_v[e, pl.ds(pl.multiple_of(32 * rem(i - fm + 4, 4), 32), 32), SPAN * c:SPAN * c + SPAN]
                for i in range(4)
            ],
            axis=0,
        )

    TAIL_BLOCKS = ((0, 1, 2, 3), (4, 5), (6, 7, 8, 9), (10, 11))

    def err_columns(tb):
        return jnp.concatenate(
            [
                e_v[b // 6, 128:160, SPAN * (b % 6):SPAN * (b % 6) + SPAN]
                for b in TAIL_BLOCKS[tb] + TAIL_BLOCKS[tb][:4 - len(TAIL_BLOCKS[tb])]
            ],
            axis=0,
        )

    def main_rows(b):
        ga = (5 * b) // 4
        return low[32 * ga:32 * ga + 64]

    def tail_rows(tb):
        gs = [b + 1 + b // 4 for b in TAIL_BLOCKS[tb]]
        return jnp.concatenate([low[32 * g:32 * g + 32] for g in gs], axis=0)

    def main_select(b, o):
        pa, pb = o[0:16] + o[16:32], o[32:48] + o[48:64]
        return jnp.where(place16 < 128 - 32 * (b % 4), pa, pb)

    def tail_select(o):
        p = o[0:16] + o[16:32]
        for j in range(1, o.shape[0] // 32):
            p = jnp.where(lane16 < 32 * j, p, o[32 * j:32 * j + 16] + o[32 * j + 16:32 * j + 32])
        return p

    for b in range(12):
        from_err[b] = 0.95 * main_select(b, dot_nt(main_rows(b), turned(b // 6, b % 6)))
    for tb in range(4):
        from_err[12 + tb] = 0.95 * tail_select(dot_nt(tail_rows(tb), err_columns(tb)))

    def take_delta(p):
        part = recv.at[p, pl.ds(0, (N - 1) * ROWS)] if p < 2 else recv_t.at[p - 2, pl.ds(0, N - 1)]
        pltpu.make_async_copy(part, part, a2a_r.at[p]).wait()

    def pick_main(e):
        take_delta(e)
        for c in range(6):
            b = 6 * e + c
            x = recv[e, SPAN * c:SPAN * c + SPAN]
            kept[b] = (main_select(b, dot(main_rows(b), x)) + from_err[b]).astype(BF16)

    def pick_tail(e):
        take_delta(2 + e)
        for tb in (2 * e, 2 * e + 1):
            for t16 in range(16):
                v = None
                for j, b in enumerate(TAIL_BLOCKS[tb]):
                    row = SPAN * (b % 6) + 16 * t16
                    i = (row % ROWS) // 16
                    w = recv_t[e, row // ROWS].astype(F32)
                    sh = (32 * (j - i)) % 128
                    w = pltpu.roll(w, sh, 1) if sh else w
                    v = w if v is None else jnp.where(lane16 < 32 * j, v, w)
                x_t[tb, 16 * t16:16 * t16 + 16] = v.astype(BF16)
        for tb in (2 * e, 2 * e + 1):
            kept[12 + tb] = (tail_select(dot(tail_rows(tb), x_t[tb])) + from_err[12 + tb]).astype(BF16)

    def tile_of(slot, b8):
        if slot == 0:
            return jnp.minimum(b8, 5)
        if slot == 1:
            return jnp.where(b8 < 4, b8 + 8, jnp.maximum(b8, 6))
        return jnp.where(b8 < 4, 12, 13)

    def send_kept(slot):
        rows = pl.ds(pl.multiple_of(16 * r, 16), 16)
        for o in range(1, R):
            pltpu.make_async_remote_copy(
                src_ref=kept.at[tile_of(slot, rem(mine_first + o, R))], dst_ref=kept_in.at[slot, rows],
                send_sem=kept_s.at[slot], recv_sem=kept_r.at[slot],
                device_id=(rem(r + o, R), f), device_id_type=MESH,
            ).start()
        pltpu.make_async_copy(
            kept.at[tile_of(slot, mine_first)], kept_in.at[slot, rows], kept_r.at[slot]
        ).start()

    def send_last():
        rows = pl.ds(pl.multiple_of(16 * r, 16), 16)
        for o in (4, 3, 5, 2, 6, 1, 7):
            pltpu.make_async_remote_copy(
                src_ref=kept.at[pl.ds(14, 2)], dst_ref=kept_last.at[:, rows],
                send_sem=kept_s.at[3], recv_sem=kept_r.at[3],
                device_id=(rem(r + o, R), f), device_id_type=MESH,
            ).start()
        for k in range(2):
            kept_last[k, rows] = kept[14 + k]

    def average_last():
        part = kept_last.at[:, pl.ds(0, 16 * (R - 1))]
        pltpu.make_async_copy(part, part, kept_r.at[3]).wait()
        into, outof = lax.broadcasted_iota(I32, (128, 128), 0), lanes((128, 128))
        ks = []
        for c in range(6):
            same = (div(into, 32) == c % 4) & (rem(into, 32) == rem(outof, 32))
            ks.append(dot(kept_last[c // 4], jnp.where(same, 1.0, 0.0).astype(BF16)).astype(BF16))
        for c in range(6):
            u_last[SPAN * c:SPAN * c + SPAN] = (
                dot(basis_last[c], jnp.concatenate([ks[c], ks[c]], axis=0)) * 0.125
            ).astype(BF16)
        for d in range(N):
            w = [u_last[ROWS * d + 16 * i:ROWS * d + 16 * i + 16] for i in range(3)]
            last_msg[d] = jnp.where(lane16 < 32, w[0], jnp.where(lane16 < 64, w[1], w[2]))
        for dy in (2, 1, 3, 0):
            for dz in (4, 3, -3, 2, -2, 1, -1, 0):
                if dy or dz:
                    d = 8 * rem(y + dy, 4) + rem(z + dz + 8, 8)
                    pltpu.make_async_remote_copy(
                        src_ref=last_msg.at[d], dst_ref=last_recv.at[f], send_sem=last_s, recv_sem=last_r,
                        device_id=(r, d), device_id_type=MESH,
                    ).start()
        last_recv[f] = last_msg[f]

    def take_last():
        part = last_recv.at[pl.ds(0, N - 1)]
        pltpu.make_async_copy(part, part, last_r).wait()
        for q in range(8):
            ws = [last_recv[4 * q + m].astype(F32) for m in range(4)]
            for i in range(3):
                v = None
                for m in range(4):
                    w = pltpu.roll(ws[m], (32 * (m - i)) % 128, 1) if m != i else ws[m]
                    v = w if v is None else jnp.where(lane16 < 32 * m, v, w)
                last_tail[q, 16 * i:16 * i + 16] = v.astype(BF16)

    def restore_main(e):
        for c in range(6):
            b = 6 * e + c
            k, zero = kept[b], jnp.zeros((16, 128), BF16)
            first = place16 < 128 - 32 * (b % 4)
            ka, kb = jnp.where(first, k, zero), jnp.where(first, zero, k)
            back = dot_tn(jnp.concatenate([ka, ka, kb, kb], axis=0), main_rows(b))
            x = recv[e, SPAN * c:SPAN * c + SPAN].astype(F32)
            en = (0.95 * turned(e, c).astype(F32) + jnp.transpose(x) - back).astype(BF16)
            for i in range(4):
                err_out[
                    e, pl.ds(pl.multiple_of(32 * rem(i - fm + 4, 4), 32), 32), SPAN * c:SPAN * c + SPAN
                ] = en[32 * i:32 * i + 32]

    def restore_tail(e):
        for tb in (2 * e, 2 * e + 1):
            k, zero = kept[12 + tb], jnp.zeros((16, 128), BF16)
            ks = []
            for j in range(len(TAIL_BLOCKS[tb])):
                kj = jnp.where((lane16 >= 32 * j) & (lane16 < 32 * j + 32), k, zero)
                ks += [kj, kj]
            back = dot_tn(jnp.concatenate(ks, axis=0), tail_rows(tb))
            en = 0.95 * err_columns(tb).astype(F32) + jnp.transpose(x_t[tb].astype(F32)) - back
            en = en.astype(BF16)
            for j, b in enumerate(TAIL_BLOCKS[tb]):
                c = b % 6
                err_out[e, 128:160, SPAN * c:SPAN * c + SPAN] = en[32 * j:32 * j + 32]

    def when(flag, body):
        if flag is None:
            body()
        else:
            pl.when(flag)(body)

    def upd_move(s, v, n, what):
        e = s % 2
        c = block_of[e] - 6 * e
        at, to, rows = PIECES[v][n]
        d = 16 * div(c, 3) + 5 * v + n
        if s < 2:
            src, dst = u_out.at[s, pl.ds(at, rows)], upd.at[s, r, y, pl.ds(to, rows)]
        else:
            src, dst = u_msg.at[e, n], u_recv.at[e, 1 if to else 0, y]
        arrived = upd_r.at[s]

        @pl.when(d != f)
        def _():
            m = pltpu.make_async_remote_copy(
                src_ref=src, dst_ref=dst, send_sem=upd_s.at[s, n], recv_sem=arrived,
                device_id=(r, d), device_id_type=MESH,
            )
            m.start() if what == "start" else m.wait_send()

        if what == "start":
            @pl.when(d == f)
            def _():
                pltpu.make_async_copy(src, dst, arrived).start()

    def upd_all(s, what):
        for v in range(3):
            @pl.when(rem(block_of[s % 2], 3) == v)
            def _():
                for n in range(6):
                    upd_move(s, v, n, what)

    def take_kept(s):
        pltpu.make_async_copy(kept_in.at[s], kept_in.at[s], kept_r.at[s]).wait()
        return kept_in[s]

    def average_main(s):
        k = take_kept(s)
        zero = jnp.zeros_like(k)
        first = place128 < 128 - 32 * rem(block_of[s], 4)
        ka = jnp.where(first, k, zero)
        kb = jnp.where(first, zero, k)
        u = dot(basis[2 * s], jnp.concatenate([ka, ka], axis=0))
        u = u + dot(basis[2 * s + 1], jnp.concatenate([kb, kb], axis=0))
        u_out[s] = (u * 0.125).astype(BF16)
        when(has_block[s], functools.partial(upd_all, s, "start"))

    def average_tail(e):
        into, outof = lax.broadcasted_iota(I32, (128, 128), 0), lanes((128, 128))
        same = (div(into, 32) == rem(block_of[e] + 2 * e, 4)) & (rem(into, 32) == rem(outof, 32))
        same = jnp.where(same, 1.0, 0.0).astype(BF16)
        k = dot(take_kept(2 + e), same).astype(BF16)
        u_tail[...] = dot(basis[4 + e], jnp.concatenate([k, k], axis=0)) * 0.125
        for v in range(3):
            @pl.when(rem(block_of[e], 3) == v)
            def _():
                for n, (at, to, rows) in enumerate(PIECES[v]):
                    w = None
                    for i in range(rows // 16):
                        x = u_tail[at + 16 * i:at + 16 * i + 16]
                        w = x if w is None else jnp.where(lane16 < to * 2 + 32 * i, w, x)
                    u_msg[e, n] = w.astype(BF16)
        when(has_block[e], functools.partial(upd_all, 2 + e, "start"))

    chunk = [div(3 * f + i, 16) for i in range(3)]

    def wait_upd(p):
        def some(part):
            pltpu.make_async_copy(part, part, upd_r.at[p]).wait()

        if p < 2:
            some(upd.at[p, 0])
            return

        @pl.when(chunk[0] == chunk[2])
        def _():
            some(u_recv.at[p - 2, 0])

        @pl.when(chunk[0] != chunk[2])
        def _():
            some(u_recv.at[p - 2])

    def fwd_copy(p, other):
        ref = upd.at[p, r] if p < 2 else upd_tail.at[r]
        return pltpu.make_async_remote_copy(
            src_ref=ref, dst_ref=ref, send_sem=fwd_s.at[p], recv_sem=fwd_r.at[p],
            device_id=(other, f), device_id_type=MESH,
        )

    def forward(p):
        wait_upd(p)
        if p >= 2:
            e = p - 2
            for i in range(3):
                whole = jnp.zeros((16, 128), F32)
                behind = div(rem(r - 6 * e - chunk[i] + 2 * R, R), 2)
                for yy in range(4):
                    m = rem(behind - yy + 4, 4)
                    v = u_recv[e, chunk[i] - chunk[0], yy].astype(F32)
                    v = pltpu.roll(v, rem(32 * (m - i) + 128, 128), 1)
                    whole = jnp.where(div(lane16, 32) == m, v, whole)
                upd_tail[r, 16 * i:16 * i + 16] = whole.astype(BF16)
        for o in range(1, R):
            fwd_copy(p, rem(r + o, R)).start()

    pick_main(0)
    send_kept(0)
    pick_tail(0)
    send_kept(2)
    restore_main(0)
    restore_tail(0)
    average_main(0)
    average_tail(0)
    groups_start(3, 0, 8)
    pick_main(1)
    send_kept(1)
    average_main(1)
    pick_tail(1)
    send_last()
    forward(0)
    forward(2)
    restore_main(1)
    average_last()
    forward(1)
    restore_tail(1)
    take_last()

    for p in range(3):
        part = upd.at[p, pl.ds(0, R - 1)] if p < 2 else upd_tail.at[pl.ds(0, R - 1)]
        pltpu.make_async_copy(part, part, fwd_r.at[p]).wait()
        pltpu.make_async_copy(part, part, fwd_s.at[p]).wait()

    for j in range(32):
        group_wait(j)
    for c in loads[6:]:
        c.wait()

    part = idx_all.at[pl.ds(0, R - 1)]
    pltpu.make_async_copy(part, part, idx_s).wait()
    for s in range(3):
        pltpu.make_async_copy(
            kept_in.at[s, pl.ds(0, 16 * (R - 1))], kept_in.at[s, pl.ds(0, 16 * (R - 1))], kept_s.at[s]
        ).wait()
    for s in range(3):
        when(has_block[s % 2], functools.partial(upd_all, s, "wait"))
    part = kept_last.at[:, pl.ds(0, 16 * (R - 1))]
    pltpu.make_async_copy(part, part, kept_s.at[3]).wait()
    part = last_msg.at[pl.ds(0, N - 1)]
    pltpu.make_async_copy(part, part, last_s).wait()


def exchange(delta, err, cos, idx, count, theta, momentum):
    vmem = pl.BlockSpec(memory_space=pltpu.VMEM)
    hbm = pl.BlockSpec(memory_space=pltpu.HBM)
    args = (delta, err, cos, idx, count, theta, momentum)
    args = [pltpu.with_memory_space_constraint(a, pltpu.HBM) for a in args]
    return pl.pallas_call(
        exchange_kernel,
        out_shape=(
            pltpu.VMEM((2, R, 4, ROWS, 128), BF16),
            pltpu.VMEM((R, ROWS, 128), BF16),
            pltpu.VMEM((8, ROWS, 128), BF16),
            pltpu.VMEM((2, 160, 1536), BF16),
            pltpu.VMEM(theta.shape, F32),
            pltpu.VMEM(theta.shape, F32),
        ),
        in_specs=[hbm] * 7,
        out_specs=(vmem,) * 6,
        scratch_shapes=[
            pltpu.VMEM((2, ROWS, 5120), BF16),
            pltpu.VMEM((2, 160, 1536), BF16),
            pltpu.VMEM((SPAN, SPAN), F32),
            pltpu.VMEM((4, SPAN, SPAN), BF16),
            pltpu.VMEM((15, 1, 16), I32),
            pltpu.SMEM((1, 15), I32),
            pltpu.VMEM((16, 128), F32),
            pltpu.VMEM((16, 128), F32),
            pltpu.VMEM((2, N, ROWS, 128), BF16),
            pltpu.VMEM((2, N, 16, 128), BF16),
            pltpu.VMEM((2, N * ROWS, 128), BF16),
            pltpu.VMEM((2, N, 16, 128), BF16),
            pltpu.VMEM((4, SPAN, 128), BF16),
            pltpu.VMEM((15 * 32, SPAN), BF16),
            pltpu.VMEM((6, SPAN, SPAN), BF16),
            pltpu.VMEM((16, 16, 128), F32),
            pltpu.VMEM((R, 16, 128), F32),
            pltpu.VMEM((16, 128), F32),
            pltpu.VMEM((16, 16, 128), BF16),
            pltpu.VMEM((4, 128, 128), BF16),
            pltpu.VMEM((2, SPAN, 128), BF16),
            pltpu.VMEM((SPAN, 128), F32),
            pltpu.VMEM((2, 6, 16, 128), BF16),
            pltpu.VMEM((2, 2, 4, 16, 128), BF16),
            pltpu.VMEM((2, 128, 128), BF16),
            pltpu.VMEM((6, SPAN, SPAN), BF16),
            pltpu.VMEM((N * ROWS, 128), BF16),
            pltpu.VMEM((N, 16, 128), BF16),
            pltpu.VMEM((N, 16, 128), BF16),
            pltpu.SemaphoreType.DMA((8,)),
            pltpu.SemaphoreType.DMA((32,)),
            pltpu.SemaphoreType.DMA((4,)),
            pltpu.SemaphoreType.DMA,
            pltpu.SemaphoreType.DMA,
            pltpu.SemaphoreType.DMA((4,)),
            pltpu.SemaphoreType.DMA((4,)),
            pltpu.SemaphoreType.DMA((4, 6)),
            pltpu.SemaphoreType.DMA((4,)),
            pltpu.SemaphoreType.DMA((4,)),
            pltpu.SemaphoreType.DMA((4,)),
            pltpu.SemaphoreType.DMA,
            pltpu.SemaphoreType.DMA,
        ],
        compiler_params=pltpu.CompilerParams(
            collective_id=0, has_side_effects=True, vmem_limit_bytes=32 << 20
        ),
        name="exchange",
    )(*args)


def finish_kernel(
    upd, upd_tail, last_tail, err, theta, momentum,
    theta_out, momentum_out, err_out,
    th, mo, err_sem, th_sem, mo_sem,
):
    moved = pltpu.make_async_copy(err, err_out, err_sem)
    moved.start()

    def write(q):
        cols = pl.ds(640 * q, 640)
        return (
            pltpu.make_async_copy(th.at[:, :, cols], theta_out.at[:, :, cols], th_sem.at[q]),
            pltpu.make_async_copy(mo.at[:, :, cols], momentum_out.at[:, :, cols], mo_sem.at[q]),
        )

    f = lax.axis_index("fsdp")
    lane = lanes((16, 128))
    for q in range(8):
        y, core = q // 2, q % 2
        for e in range(2):
            for i in range(3):
                rows = slice(16 * i, 16 * i + 16)
                shift = 6 * e + div(3 * f + i, 16) + core
                reps = [rem(shift + 2 * ((y + m) % 4), R) for m in range(4)]
                main = [upd[e, reps[m], y, rows].astype(F32) for m in range(4)]
                if e == 0:
                    tail = [upd_tail[reps[m], rows].astype(F32) for m in range(4)]
                else:
                    tail = [last_tail[q, rows].astype(F32)] * 4
                tiles = [
                    main[0],
                    jnp.where(lane < 32, tail[0], main[1]),
                    jnp.where(lane < 32, main[1], jnp.where(lane < 64, tail[1], main[2])),
                    jnp.where(lane < 64, main[2], jnp.where(lane < 96, tail[2], main[3])),
                    jnp.where(lane < 96, main[3], tail[3]),
                ]
                for k in range(5):
                    cols = slice(640 * q + 128 * k, 640 * q + 128 * k + 128)
                    m_new = 0.9 * momentum[e, rows, cols] + tiles[k]
                    mo[e, rows, cols] = m_new
                    th[e, rows, cols] = theta[e, rows, cols] - 0.7 * (tiles[k] + 0.9 * m_new)
        for c in write(q):
            c.start()
    for q in range(8):
        for c in write(q):
            c.wait()
    moved.wait()


def finish(*args):
    vmem = pl.BlockSpec(memory_space=pltpu.VMEM)
    hbm = pl.BlockSpec(memory_space=pltpu.HBM)
    err, theta = args[3], args[4]
    args = [pltpu.with_memory_space_constraint(a, pltpu.VMEM) for a in args]
    return pl.pallas_call(
        finish_kernel,
        out_shape=(
            jax.ShapeDtypeStruct(theta.shape, F32),
            jax.ShapeDtypeStruct(theta.shape, F32),
            jax.ShapeDtypeStruct(err.shape, BF16),
        ),
        in_specs=[vmem] * 6,
        out_specs=(hbm, hbm, hbm),
        scratch_shapes=[
            pltpu.VMEM((2, ROWS, 5120), F32),
            pltpu.VMEM((2, ROWS, 5120), F32),
            pltpu.SemaphoreType.DMA,
            pltpu.SemaphoreType.DMA((8,)),
            pltpu.SemaphoreType.DMA((8,)),
        ],
        compiler_params=pltpu.CompilerParams(vmem_limit_bytes=16 << 20),
        name="finish",
    )(*args)


def shards(delta, error, theta, momentum, block_index, block_count):
    cos = jnp.asarray(cosine_table())
    err = jnp.transpose(error[0], (0, 2, 1))
    idx = block_index.reshape(15, 1, 16)
    made = exchange(delta[0], err, cos, idx, block_count, theta, momentum)
    theta_new, momentum_new, err_new = finish(*made)
    return theta_new, momentum_new, jnp.transpose(err_new, (0, 2, 1))[None]


def solution(mesh):
    return jax.shard_map(
        shards,
        mesh=mesh,
        in_specs=(
            P("replica", None, "fsdp", None),
            P("replica", None, None, "fsdp"),
            P(None, "fsdp", None),
            P(None, "fsdp", None),
            P("replica", "fsdp", None),
            P("replica", "fsdp"),
        ),
        out_specs=(P(None, "fsdp", None), P(None, "fsdp", None), P("replica", None, None, "fsdp")),
        check_vma=False,
    )
```

```python
import functools

import jax
import jax.numpy as jnp
import numpy as np
from jax import lax
from jax.experimental import pallas as pl
from jax.experimental.pallas import tpu as pltpu
from jax.sharding import PartitionSpec as P

SPAN = 256
N = 32
R = 8
ROWS = 48
MESH = pl.DeviceIdType.MESH
F32 = jnp.float32
BF16 = jnp.bfloat16
I32 = jnp.int32


def cosine_table():
    k = np.arange(SPAN, dtype=np.float64)[:, None]
    t = np.arange(SPAN, dtype=np.float64)[None, :]
    m = np.cos(np.pi * (2.0 * t + 1.0) * k / (2.0 * SPAN))
    return (m * np.where(k == 0, np.sqrt(1.0 / SPAN), np.sqrt(2.0 / SPAN))).astype(np.float32)


def div(a, b):
    return lax.div(a, jnp.int32(b))


def rem(a, b):
    return lax.rem(a, jnp.int32(b))


def turn_of(f):
    y, z = div(f, 8), rem(f, 8)
    return 2 * rem(y + z, 4) + div(z, 4)


PIECES = (
    [(48 * n, 0, 48) for n in range(5)] + [(240, 0, 16)],
    [(0, 16, 32)] + [(32 + 48 * n, 0, 48) for n in range(4)] + [(224, 0, 32)],
    [(0, 32, 16)] + [(16 + 48 * n, 0, 48) for n in range(5)],
)


def dot_nt(a, b):
    return lax.dot_general(a, b, (((1,), (1,)), ((), ())), preferred_element_type=F32)


def dot_tn(a, b):
    return lax.dot_general(a, b, (((0,), (0,)), ((), ())), preferred_element_type=F32)


def dot(a, b):
    return jnp.dot(a, b, preferred_element_type=F32)


def lanes(shape):
    return lax.broadcasted_iota(I32, shape, len(shape) - 1)


def exchange_kernel(
    delta, err, cos, idx, count, theta, momentum,
    upd, upd_tail, last_tail, err_out, theta_v, momentum_v,
    d_v, e_v, table, cos_v, idx_v, count_s, lists, own_idx, send, send_t, recv, recv_t, x_t, low, basis,
    from_err, idx_all, merged, kept, kept_in, u_out, u_tail, u_msg, u_recv,
    kept_last, basis_last, u_last, last_msg, last_recv,
    load_sem, a2a_s, a2a_r, idx_s, idx_r, kept_s, kept_r, upd_s, upd_r, fwd_s, fwd_r, last_s, last_r,
):
    r = lax.axis_index("replica")
    f = lax.axis_index("fsdp")
    y, z = div(f, 8), rem(f, 8)
    fm = rem(f, 4)
    turn = turn_of(f)
    mine_first = rem(r - turn + R, R)
    block_of = (mine_first, jnp.where(mine_first < 4, mine_first + 8, mine_first))
    has_block = (mine_first < 6, (mine_first < 4) | (mine_first >= 6))

    loads = [
        pltpu.make_async_copy(delta.at[0], d_v.at[0], load_sem.at[0]),
        pltpu.make_async_copy(delta.at[1], d_v.at[1], load_sem.at[1]),
        pltpu.make_async_copy(cos, table, load_sem.at[2]),
        pltpu.make_async_copy(err, e_v, load_sem.at[3]),
        pltpu.make_async_copy(idx, idx_v, load_sem.at[4]),
        pltpu.make_async_copy(count, count_s, load_sem.at[5]),
        pltpu.make_async_copy(theta, theta_v, load_sem.at[6]),
        pltpu.make_async_copy(momentum, momentum_v, load_sem.at[7]),
    ]
    loads[0].start()

    bar = pltpu.get_barrier_semaphore()

    for dy in (2, 1, 3, 0):
        for dz in (4, 3, -3, 2, -2, 1, -1, 0):
            if dy or dz:
                d = 8 * rem(y + dy, 4) + rem(z + dz + 8, 8)
                pl.semaphore_signal(bar, inc=1, device_id=(r, d), device_id_type=MESH)
    for o in (4, 3, 5, 2, 6, 1, 7):
        pl.semaphore_signal(bar, inc=1, device_id=(rem(r + o, R), f), device_id_type=MESH)
    for c in loads[1:6]:
        c.start()

    lane16 = lanes((16, 128))

    def pack_main(e):
        def body(q, _):
            for i in range(3):
                rows = pl.ds(16 * i, 16)
                t = [
                    d_v[e, rows, pl.ds(pl.multiple_of(640 * q + 128 * k, 128), 128)]
                    for k in range(5)
                ]
                send[e, 4 * q, rows] = t[0]
                send[e, 4 * q + 1, rows] = jnp.where(lane16 >= 32, t[1], t[2])
                send[e, 4 * q + 2, rows] = jnp.where(lane16 >= 64, t[2], t[3])
                send[e, 4 * q + 3, rows] = jnp.where(lane16 >= 96, t[3], t[4])
            return 0

        lax.fori_loop(0, 8, body, 0)

    def pack_tail(e):
        def body(q, _):
            zs = []
            for i in range(3):
                t = [
                    d_v[e, 16 * i:16 * i + 16, pl.ds(pl.multiple_of(640 * q + 128 * k, 128), 128)]
                    for k in range(1, 5)
                ]
                v = jnp.where(
                    lane16 < 32, t[0], jnp.where(lane16 < 64, t[1], jnp.where(lane16 < 96, t[2], t[3]))
                )
                zs.append(v.astype(F32))
            for m in range(4):
                w = None
                for i in range(3):
                    s = (32 * (i - m)) % 128
                    v = pltpu.roll(zs[i], s, 1) if s else zs[i]
                    w = v if w is None else jnp.where(lane16 < 32 * i, w, v)
                send_t[e, 4 * q + m] = w.astype(BF16)
            return 0

        lax.fori_loop(0, 8, body, 0)

    def offsets(half, dy):
        turns = ((3, -3, 4, -2), (2, 1, -1, 0))[half]
        return [((2, 1, 3, 0)[dy], dz) for dz in turns if (2, 1, 3, 0)[dy] or dz]

    def group_ref(j):
        n = len(offsets(j % 2, j % 8 // 2))
        return send.at[0, pl.ds(0, n)] if j < 16 else send_t.at[0, pl.ds(0, n)]

    def group_start(j):
        p = j // 8
        for dy, dz in offsets(j % 2, j % 8 // 2):
            d = 8 * rem(y + dy, 4) + rem(z + dz + 8, 8)
            if p < 2:
                src, dst = send.at[p, d], recv.at[p, pl.ds(pl.multiple_of(ROWS * f, 16), ROWS)]
            else:
                src, dst = send_t.at[p - 2, d], recv_t.at[p - 2, f]
            pltpu.make_async_remote_copy(
                src_ref=src, dst_ref=dst, send_sem=a2a_s.at[j], recv_sem=a2a_r.at[p],
                device_id=(r, d), device_id_type=MESH,
            ).start()

    def group_wait(j):
        pltpu.make_async_copy(group_ref(j), group_ref(j), a2a_s.at[j]).wait()

    def groups_start(p, first, last):
        for j in range(8 * p + first, 8 * p + last):
            group_start(j)

    loads[0].wait()
    pack_main(0)
    pl.semaphore_wait(bar, N - 1 + R - 1)
    groups_start(0, 0, 8)
    pack_tail(0)
    groups_start(2, 0, 8)
    loads[1].wait()
    pack_main(1)
    groups_start(1, 0, 8)
    pack_tail(1)
    for c in loads[6:]:
        c.start()
    for e in range(2):
        recv[e, pl.ds(pl.multiple_of(ROWS * f, 16), ROWS)] = send[e, f]
        recv_t[e, f] = send_t[e, f]

    loads[4].wait()
    loads[5].wait()
    lists[...] = jnp.full((16, 128), -1.0, F32)
    for g in range(15):
        named = jnp.where(lanes((1, 16)) < count_s[0, g], idx_v[g], -1)
        lists[g:g + 1, 0:16] = named.astype(F32)
    held = lists[...].astype(BF16)
    into, outof = lax.broadcasted_iota(I32, (128, 128), 0), lanes((128, 128))
    spread = jnp.where((into < 16) & (rem(outof, 16) == into), 1.0, 0.0).astype(BF16)
    own_idx[...] = dot(held, spread)

    idx_all[r] = own_idx[...]
    for o in range(1, R):
        pltpu.make_async_remote_copy(
            src_ref=own_idx, dst_ref=idx_all.at[r],
            send_sem=idx_s, recv_sem=idx_r, device_id=(rem(r + o, R), f), device_id_type=MESH,
        ).start()

    loads[2].wait()
    for way, full in enumerate((table[...], jnp.transpose(table[...]))):
        high = full.astype(BF16)
        cos_v[2 * way] = high
        cos_v[2 * way + 1] = (full - high.astype(F32)).astype(BF16)
    slot, group = lax.broadcasted_iota(I32, (SPAN, 16), 0), lanes((SPAN, 16))
    mine = dot(jnp.where(div(slot, 16) == group, 1.0, 0.0).astype(BF16), held)
    slot, lane = lax.broadcasted_iota(I32, (SPAN, 128), 0), lanes((SPAN, 128))
    mine = jnp.where(rem(slot, 16) == lane, mine, 0.0).astype(BF16)
    mine = dot(mine, jnp.ones((128, SPAN), BF16))
    pick = jnp.where(mine == lanes((SPAN, SPAN)).astype(F32), 1.0, 0.0).astype(BF16)
    for part in range(2):
        rows = dot(pick, cos_v[part]).astype(BF16)
        for g in range(15):
            low[32 * g + 16 * part:32 * g + 16 * part + 16] = rows[16 * g:16 * g + 16]

    part = idx_all.at[pl.ds(0, R - 1)]
    pltpu.make_async_copy(part, part, idx_r).wait()
    lists_all = idx_all[0]
    for p in range(1, R):
        lists_all = jnp.where(lane16 < 16 * p, lists_all, idx_all[p])
    merged[...] = lists_all
    kk = lax.broadcasted_iota(I32, (SPAN, 128), 0).astype(F32)
    first_a, first_b = div(5 * block_of[0], 4), div(5 * block_of[1], 4)
    first_a = jnp.minimum(first_a, 13)
    tail_a = block_of[0] + 1 + div(block_of[0], 4)
    def fill(to, g):
        hot = jnp.where(kk == merged[pl.ds(g, 1), :], 1.0, 0.0).astype(BF16)
        to[:, 0:128] = dot(cos_v[2], hot).astype(BF16)
        to[:, 128:256] = dot(cos_v[3], hot).astype(BF16)

    for s, g in enumerate((first_a, first_a + 1, first_b, first_b + 1, tail_a)):
        fill(basis.at[s], g)
    for c in range(6):
        fill(basis_last.at[c], c + 7 + (c + 6) // 4)

    loads[3].wait()

    place16 = rem(lane16 - 32 * fm + 128, 128)
    place128 = rem(lanes((128, 128)) - 32 * fm + 128, 128)

    def turned(e, c):
        return jnp.concatenate(
            [
                e_v[e, pl.ds(pl.multiple_of(32 * rem(i - fm + 4, 4), 32), 32), SPAN * c:SPAN * c + SPAN]
                for i in range(4)
            ],
            axis=0,
        )

    TAIL_BLOCKS = ((0, 1, 2, 3), (4, 5), (6, 7, 8, 9), (10, 11))

    def err_columns(tb):
        return jnp.concatenate(
            [
                e_v[b // 6, 128:160, SPAN * (b % 6):SPAN * (b % 6) + SPAN]
                for b in TAIL_BLOCKS[tb] + TAIL_BLOCKS[tb][:4 - len(TAIL_BLOCKS[tb])]
            ],
            axis=0,
        )

    def main_rows(b):
        ga = (5 * b) // 4
        return low[32 * ga:32 * ga + 64]

    def tail_rows(tb):
        gs = [b + 1 + b // 4 for b in TAIL_BLOCKS[tb]]
        return jnp.concatenate([low[32 * g:32 * g + 32] for g in gs], axis=0)

    def main_select(b, o):
        pa, pb = o[0:16] + o[16:32], o[32:48] + o[48:64]
        return jnp.where(place16 < 128 - 32 * (b % 4), pa, pb)

    def tail_select(o):
        p = o[0:16] + o[16:32]
        for j in range(1, o.shape[0] // 32):
            p = jnp.where(lane16 < 32 * j, p, o[32 * j:32 * j + 16] + o[32 * j + 16:32 * j + 32])
        return p

    for b in range(12):
        from_err[b] = 0.95 * main_select(b, dot_nt(main_rows(b), turned(b // 6, b % 6)))
    for tb in range(4):
        from_err[12 + tb] = 0.95 * tail_select(dot_nt(tail_rows(tb), err_columns(tb)))

    def take_delta(p):
        part = recv.at[p, pl.ds(0, (N - 1) * ROWS)] if p < 2 else recv_t.at[p - 2, pl.ds(0, N - 1)]
        pltpu.make_async_copy(part, part, a2a_r.at[p]).wait()

    def pick_main(e):
        take_delta(e)
        for c in range(6):
            b = 6 * e + c
            x = recv[e, SPAN * c:SPAN * c + SPAN]
            kept[b] = (main_select(b, dot(main_rows(b), x)) + from_err[b]).astype(BF16)

    def pick_tail(e):
        take_delta(2 + e)
        for tb in (2 * e, 2 * e + 1):
            for t16 in range(16):
                v = None
                for j, b in enumerate(TAIL_BLOCKS[tb]):
                    row = SPAN * (b % 6) + 16 * t16
                    i = (row % ROWS) // 16
                    w = recv_t[e, row // ROWS].astype(F32)
                    sh = (32 * (j - i)) % 128
                    w = pltpu.roll(w, sh, 1) if sh else w
                    v = w if v is None else jnp.where(lane16 < 32 * j, v, w)
                x_t[tb, 16 * t16:16 * t16 + 16] = v.astype(BF16)
        for tb in (2 * e, 2 * e + 1):
            kept[12 + tb] = (tail_select(dot(tail_rows(tb), x_t[tb])) + from_err[12 + tb]).astype(BF16)

    def tile_of(slot, b8):
        if slot == 0:
            return jnp.minimum(b8, 5)
        if slot == 1:
            return jnp.where(b8 < 4, b8 + 8, jnp.maximum(b8, 6))
        return jnp.where(b8 < 4, 12, 13)

    def send_kept(slot):
        rows = pl.ds(pl.multiple_of(16 * r, 16), 16)
        for o in range(1, R):
            pltpu.make_async_remote_copy(
                src_ref=kept.at[tile_of(slot, rem(mine_first + o, R))], dst_ref=kept_in.at[slot, rows],
                send_sem=kept_s.at[slot], recv_sem=kept_r.at[slot],
                device_id=(rem(r + o, R), f), device_id_type=MESH,
            ).start()
        pltpu.make_async_copy(
            kept.at[tile_of(slot, mine_first)], kept_in.at[slot, rows], kept_r.at[slot]
        ).start()

    def send_last():
        rows = pl.ds(pl.multiple_of(16 * r, 16), 16)
        for o in (4, 3, 5, 2, 6, 1, 7):
            pltpu.make_async_remote_copy(
                src_ref=kept.at[pl.ds(14, 2)], dst_ref=kept_last.at[:, rows],
                send_sem=kept_s.at[3], recv_sem=kept_r.at[3],
                device_id=(rem(r + o, R), f), device_id_type=MESH,
            ).start()
        for k in range(2):
            kept_last[k, rows] = kept[14 + k]

    def average_last():
        part = kept_last.at[:, pl.ds(0, 16 * (R - 1))]
        pltpu.make_async_copy(part, part, kept_r.at[3]).wait()
        into, outof = lax.broadcasted_iota(I32, (128, 128), 0), lanes((128, 128))
        ks = []
        for c in range(6):
            same = (div(into, 32) == c % 4) & (rem(into, 32) == rem(outof, 32))
            ks.append(dot(kept_last[c // 4], jnp.where(same, 1.0, 0.0).astype(BF16)).astype(BF16))
        for c in range(6):
            u_last[SPAN * c:SPAN * c + SPAN] = (
                dot(basis_last[c], jnp.concatenate([ks[c], ks[c]], axis=0)) * 0.125
            ).astype(BF16)
        for d in range(N):
            w = [u_last[ROWS * d + 16 * i:ROWS * d + 16 * i + 16] for i in range(3)]
            last_msg[d] = jnp.where(lane16 < 32, w[0], jnp.where(lane16 < 64, w[1], w[2]))
        for dy in (2, 1, 3, 0):
            for dz in (4, 3, -3, 2, -2, 1, -1, 0):
                if dy or dz:
                    d = 8 * rem(y + dy, 4) + rem(z + dz + 8, 8)
                    pltpu.make_async_remote_copy(
                        src_ref=last_msg.at[d], dst_ref=last_recv.at[f], send_sem=last_s, recv_sem=last_r,
                        device_id=(r, d), device_id_type=MESH,
                    ).start()
        last_recv[f] = last_msg[f]

    def take_last():
        part = last_recv.at[pl.ds(0, N - 1)]
        pltpu.make_async_copy(part, part, last_r).wait()
        for q in range(8):
            ws = [last_recv[4 * q + m].astype(F32) for m in range(4)]
            for i in range(3):
                v = None
                for m in range(4):
                    w = pltpu.roll(ws[m], (32 * (m - i)) % 128, 1) if m != i else ws[m]
                    v = w if v is None else jnp.where(lane16 < 32 * m, v, w)
                last_tail[q, 16 * i:16 * i + 16] = v.astype(BF16)

    def restore_main(e):
        for c in range(6):
            b = 6 * e + c
            k, zero = kept[b], jnp.zeros((16, 128), BF16)
            first = place16 < 128 - 32 * (b % 4)
            ka, kb = jnp.where(first, k, zero), jnp.where(first, zero, k)
            back = dot_tn(jnp.concatenate([ka, ka, kb, kb], axis=0), main_rows(b))
            x = recv[e, SPAN * c:SPAN * c + SPAN].astype(F32)
            en = (0.95 * turned(e, c).astype(F32) + jnp.transpose(x) - back).astype(BF16)
            for i in range(4):
                err_out[
                    e, pl.ds(pl.multiple_of(32 * rem(i - fm + 4, 4), 32), 32), SPAN * c:SPAN * c + SPAN
                ] = en[32 * i:32 * i + 32]

    def restore_tail(e):
        for tb in (2 * e, 2 * e + 1):
            k, zero = kept[12 + tb], jnp.zeros((16, 128), BF16)
            ks = []
            for j in range(len(TAIL_BLOCKS[tb])):
                kj = jnp.where((lane16 >= 32 * j) & (lane16 < 32 * j + 32), k, zero)
                ks += [kj, kj]
            back = dot_tn(jnp.concatenate(ks, axis=0), tail_rows(tb))
            en = 0.95 * err_columns(tb).astype(F32) + jnp.transpose(x_t[tb].astype(F32)) - back
            en = en.astype(BF16)
            for j, b in enumerate(TAIL_BLOCKS[tb]):
                c = b % 6
                err_out[e, 128:160, SPAN * c:SPAN * c + SPAN] = en[32 * j:32 * j + 32]

    def when(flag, body):
        if flag is None:
            body()
        else:
            pl.when(flag)(body)

    def upd_move(s, v, n, what):
        e = s % 2
        c = block_of[e] - 6 * e
        at, to, rows = PIECES[v][n]
        d = 16 * div(c, 3) + 5 * v + n
        if s < 2:
            src, dst = u_out.at[s, pl.ds(at, rows)], upd.at[s, r, y, pl.ds(to, rows)]
        else:
            src, dst = u_msg.at[e, n], u_recv.at[e, 1 if to else 0, y]
        arrived = upd_r.at[s]

        @pl.when(d != f)
        def _():
            m = pltpu.make_async_remote_copy(
                src_ref=src, dst_ref=dst, send_sem=upd_s.at[s, n], recv_sem=arrived,
                device_id=(r, d), device_id_type=MESH,
            )
            m.start() if what == "start" else m.wait_send()

        if what == "start":
            @pl.when(d == f)
            def _():
                pltpu.make_async_copy(src, dst, arrived).start()

    def upd_all(s, what):
        for v in range(3):
            @pl.when(rem(block_of[s % 2], 3) == v)
            def _():
                for n in range(6):
                    upd_move(s, v, n, what)

    def take_kept(s):
        pltpu.make_async_copy(kept_in.at[s], kept_in.at[s], kept_r.at[s]).wait()
        return kept_in[s]

    def average_main(s):
        k = take_kept(s)
        zero = jnp.zeros_like(k)
        first = place128 < 128 - 32 * rem(block_of[s], 4)
        ka = jnp.where(first, k, zero)
        kb = jnp.where(first, zero, k)
        u = dot(basis[2 * s], jnp.concatenate([ka, ka], axis=0))
        u = u + dot(basis[2 * s + 1], jnp.concatenate([kb, kb], axis=0))
        u_out[s] = (u * 0.125).astype(BF16)
        when(has_block[s], functools.partial(upd_all, s, "start"))

    def average_tail(e):
        into, outof = lax.broadcasted_iota(I32, (128, 128), 0), lanes((128, 128))
        same = (div(into, 32) == rem(block_of[e] + 2 * e, 4)) & (rem(into, 32) == rem(outof, 32))
        same = jnp.where(same, 1.0, 0.0).astype(BF16)
        k = dot(take_kept(2 + e), same).astype(BF16)
        u_tail[...] = dot(basis[4 + e], jnp.concatenate([k, k], axis=0)) * 0.125
        for v in range(3):
            @pl.when(rem(block_of[e], 3) == v)
            def _():
                for n, (at, to, rows) in enumerate(PIECES[v]):
                    w = None
                    for i in range(rows // 16):
                        x = u_tail[at + 16 * i:at + 16 * i + 16]
                        w = x if w is None else jnp.where(lane16 < to * 2 + 32 * i, w, x)
                    u_msg[e, n] = w.astype(BF16)
        when(has_block[e], functools.partial(upd_all, 2 + e, "start"))

    chunk = [div(3 * f + i, 16) for i in range(3)]

    def wait_upd(p):
        def some(part):
            pltpu.make_async_copy(part, part, upd_r.at[p]).wait()

        if p < 2:
            some(upd.at[p, 0])
            return

        @pl.when(chunk[0] == chunk[2])
        def _():
            some(u_recv.at[p - 2, 0])

        @pl.when(chunk[0] != chunk[2])
        def _():
            some(u_recv.at[p - 2])

    def fwd_copy(p, other):
        ref = upd.at[p, r] if p < 2 else upd_tail.at[r]
        return pltpu.make_async_remote_copy(
            src_ref=ref, dst_ref=ref, send_sem=fwd_s.at[p], recv_sem=fwd_r.at[p],
            device_id=(other, f), device_id_type=MESH,
        )

    def forward(p):
        wait_upd(p)
        if p >= 2:
            e = p - 2
            for i in range(3):
                whole = jnp.zeros((16, 128), F32)
                behind = div(rem(r - 6 * e - chunk[i] + 2 * R, R), 2)
                for yy in range(4):
                    m = rem(behind - yy + 4, 4)
                    v = u_recv[e, chunk[i] - chunk[0], yy].astype(F32)
                    v = pltpu.roll(v, rem(32 * (m - i) + 128, 128), 1)
                    whole = jnp.where(div(lane16, 32) == m, v, whole)
                upd_tail[r, 16 * i:16 * i + 16] = whole.astype(BF16)
        for o in range(1, R):
            fwd_copy(p, rem(r + o, R)).start()

    pick_main(0)
    send_kept(0)
    pick_tail(0)
    send_kept(2)
    restore_main(0)
    restore_tail(0)
    groups_start(3, 0, 8)
    average_main(0)
    average_tail(0)
    pick_main(1)
    send_kept(1)
    average_main(1)
    pick_tail(1)
    send_last()
    forward(0)
    forward(2)
    restore_main(1)
    average_last()
    forward(1)
    restore_tail(1)
    take_last()

    for p in range(3):
        part = upd.at[p, pl.ds(0, R - 1)] if p < 2 else upd_tail.at[pl.ds(0, R - 1)]
        pltpu.make_async_copy(part, part, fwd_r.at[p]).wait()
        pltpu.make_async_copy(part, part, fwd_s.at[p]).wait()

    for j in range(32):
        group_wait(j)
    for c in loads[6:]:
        c.wait()

    part = idx_all.at[pl.ds(0, R - 1)]
    pltpu.make_async_copy(part, part, idx_s).wait()
    for s in range(3):
        pltpu.make_async_copy(
            kept_in.at[s, pl.ds(0, 16 * (R - 1))], kept_in.at[s, pl.ds(0, 16 * (R - 1))], kept_s.at[s]
        ).wait()
    for s in range(3):
        when(has_block[s % 2], functools.partial(upd_all, s, "wait"))
    part = kept_last.at[:, pl.ds(0, 16 * (R - 1))]
    pltpu.make_async_copy(part, part, kept_s.at[3]).wait()
    part = last_msg.at[pl.ds(0, N - 1)]
    pltpu.make_async_copy(part, part, last_s).wait()


def exchange(delta, err, cos, idx, count, theta, momentum):
    vmem = pl.BlockSpec(memory_space=pltpu.VMEM)
    hbm = pl.BlockSpec(memory_space=pltpu.HBM)
    args = (delta, err, cos, idx, count, theta, momentum)
    args = [pltpu.with_memory_space_constraint(a, pltpu.HBM) for a in args]
    return pl.pallas_call(
        exchange_kernel,
        out_shape=(
            pltpu.VMEM((2, R, 4, ROWS, 128), BF16),
            pltpu.VMEM((R, ROWS, 128), BF16),
            pltpu.VMEM((8, ROWS, 128), BF16),
            pltpu.VMEM((2, 160, 1536), BF16),
            pltpu.VMEM(theta.shape, F32),
            pltpu.VMEM(theta.shape, F32),
        ),
        in_specs=[hbm] * 7,
        out_specs=(vmem,) * 6,
        scratch_shapes=[
            pltpu.VMEM((2, ROWS, 5120), BF16),
            pltpu.VMEM((2, 160, 1536), BF16),
            pltpu.VMEM((SPAN, SPAN), F32),
            pltpu.VMEM((4, SPAN, SPAN), BF16),
            pltpu.VMEM((15, 1, 16), I32),
            pltpu.SMEM((1, 15), I32),
            pltpu.VMEM((16, 128), F32),
            pltpu.VMEM((16, 128), F32),
            pltpu.VMEM((2, N, ROWS, 128), BF16),
            pltpu.VMEM((2, N, 16, 128), BF16),
            pltpu.VMEM((2, N * ROWS, 128), BF16),
            pltpu.VMEM((2, N, 16, 128), BF16),
            pltpu.VMEM((4, SPAN, 128), BF16),
            pltpu.VMEM((15 * 32, SPAN), BF16),
            pltpu.VMEM((6, SPAN, SPAN), BF16),
            pltpu.VMEM((16, 16, 128), F32),
            pltpu.VMEM((R, 16, 128), F32),
            pltpu.VMEM((16, 128), F32),
            pltpu.VMEM((16, 16, 128), BF16),
            pltpu.VMEM((4, 128, 128), BF16),
            pltpu.VMEM((2, SPAN, 128), BF16),
            pltpu.VMEM((SPAN, 128), F32),
            pltpu.VMEM((2, 6, 16, 128), BF16),
            pltpu.VMEM((2, 2, 4, 16, 128), BF16),
            pltpu.VMEM((2, 128, 128), BF16),
            pltpu.VMEM((6, SPAN, SPAN), BF16),
            pltpu.VMEM((N * ROWS, 128), BF16),
            pltpu.VMEM((N, 16, 128), BF16),
            pltpu.VMEM((N, 16, 128), BF16),
            pltpu.SemaphoreType.DMA((8,)),
            pltpu.SemaphoreType.DMA((32,)),
            pltpu.SemaphoreType.DMA((4,)),
            pltpu.SemaphoreType.DMA,
            pltpu.SemaphoreType.DMA,
            pltpu.SemaphoreType.DMA((4,)),
            pltpu.SemaphoreType.DMA((4,)),
            pltpu.SemaphoreType.DMA((4, 6)),
            pltpu.SemaphoreType.DMA((4,)),
            pltpu.SemaphoreType.DMA((4,)),
            pltpu.SemaphoreType.DMA((4,)),
            pltpu.SemaphoreType.DMA,
            pltpu.SemaphoreType.DMA,
        ],
        compiler_params=pltpu.CompilerParams(
            collective_id=0, has_side_effects=True, vmem_limit_bytes=32 << 20
        ),
        name="exchange",
    )(*args)


def finish_kernel(
    upd, upd_tail, last_tail, err, theta, momentum,
    theta_out, momentum_out, err_out,
    th, mo, err_sem, th_sem, mo_sem,
):
    moved = pltpu.make_async_copy(err, err_out, err_sem)
    moved.start()

    def write(q):
        cols = pl.ds(640 * q, 640)
        return (
            pltpu.make_async_copy(th.at[:, :, cols], theta_out.at[:, :, cols], th_sem.at[q]),
            pltpu.make_async_copy(mo.at[:, :, cols], momentum_out.at[:, :, cols], mo_sem.at[q]),
        )

    f = lax.axis_index("fsdp")
    lane = lanes((16, 128))
    for q in range(8):
        y, core = q // 2, q % 2
        for e in range(2):
            for i in range(3):
                rows = slice(16 * i, 16 * i + 16)
                shift = 6 * e + div(3 * f + i, 16) + core
                reps = [rem(shift + 2 * ((y + m) % 4), R) for m in range(4)]
                main = [upd[e, reps[m], y, rows].astype(F32) for m in range(4)]
                if e == 0:
                    tail = [upd_tail[reps[m], rows].astype(F32) for m in range(4)]
                else:
                    tail = [last_tail[q, rows].astype(F32)] * 4
                tiles = [
                    main[0],
                    jnp.where(lane < 32, tail[0], main[1]),
                    jnp.where(lane < 32, main[1], jnp.where(lane < 64, tail[1], main[2])),
                    jnp.where(lane < 64, main[2], jnp.where(lane < 96, tail[2], main[3])),
                    jnp.where(lane < 96, main[3], tail[3]),
                ]
                for k in range(5):
                    cols = slice(640 * q + 128 * k, 640 * q + 128 * k + 128)
                    m_new = 0.9 * momentum[e, rows, cols] + tiles[k]
                    mo[e, rows, cols] = m_new
                    th[e, rows, cols] = theta[e, rows, cols] - 0.7 * (tiles[k] + 0.9 * m_new)
        for c in write(q):
            c.start()
    for q in range(8):
        for c in write(q):
            c.wait()
    moved.wait()


def finish(*args):
    vmem = pl.BlockSpec(memory_space=pltpu.VMEM)
    hbm = pl.BlockSpec(memory_space=pltpu.HBM)
    err, theta = args[3], args[4]
    args = [pltpu.with_memory_space_constraint(a, pltpu.VMEM) for a in args]
    return pl.pallas_call(
        finish_kernel,
        out_shape=(
            jax.ShapeDtypeStruct(theta.shape, F32),
            jax.ShapeDtypeStruct(theta.shape, F32),
            jax.ShapeDtypeStruct(err.shape, BF16),
        ),
        in_specs=[vmem] * 6,
        out_specs=(hbm, hbm, hbm),
        scratch_shapes=[
            pltpu.VMEM((2, ROWS, 5120), F32),
            pltpu.VMEM((2, ROWS, 5120), F32),
            pltpu.SemaphoreType.DMA,
            pltpu.SemaphoreType.DMA((8,)),
            pltpu.SemaphoreType.DMA((8,)),
        ],
        compiler_params=pltpu.CompilerParams(vmem_limit_bytes=16 << 20),
        name="finish",
    )(*args)


def shards(delta, error, theta, momentum, block_index, block_count):
    cos = jnp.asarray(cosine_table())
    err = jnp.transpose(error[0], (0, 2, 1))
    idx = block_index.reshape(15, 1, 16)
    made = exchange(delta[0], err, cos, idx, block_count, theta, momentum)
    theta_new, momentum_new, err_new = finish(*made)
    return theta_new, momentum_new, jnp.transpose(err_new, (0, 2, 1))[None]


def solution(mesh):
    return jax.shard_map(
        shards,
        mesh=mesh,
        in_specs=(
            P("replica", None, "fsdp", None),
            P("replica", None, None, "fsdp"),
            P(None, "fsdp", None),
            P(None, "fsdp", None),
            P("replica", "fsdp", None),
            P("replica", "fsdp"),
        ),
        out_specs=(P(None, "fsdp", None), P(None, "fsdp", None), P("replica", None, None, "fsdp")),
        check_vma=False,
    )
```
